32 devices in a mesh: req: 16 (over z, y, x), tp: 2 (over core).
Axes of the slice: x: 2, y: 2, z: 4, core: 2. Of those that a mesh axis runs over, the one named last changes fastest.
Arguments:
- queries: bfloat16 [16, 28, 4096], P('req', None, 'tp'), may hold values from -25 to 25
- tree_kv: bfloat16 [16, 28, 2048], P('req', None, 'tp'), may hold values from -4 to 4
- tree_parent: int32 [16, 28], P('req'), may hold values from -1 to 26, as said below
- accepted_path: int32 [16, 8], replicated, may hold values from -1 to 27, as said below
- cache_kv: bfloat16 [48, 256, 2048], P('req', None, 'tp'), may hold values from -6 to 6
- piece_owner: int32 [48, 2], P('req'), may hold values from -1 to 15, as said below
- cache_len: int32 [16], replicated, may hold values from 1 to 1016, as said below
- out_weight: bfloat16 [4096, 4096], P('tp', 'req'), may hold values from -0.09375 to 0.09375
Outputs:
- mixed: bfloat16 [16, 28, 4096], P('tp', None, 'req')
- cache_out: bfloat16 [48, 256, 2048], P('req', None, 'tp')
The draws below stay inside these ranges and needn't reach their ends.
Inputs may be any that keep to these rules, and one draw needn't show every extreme that they name: tree_parent[r, 0] = -1 and 0 <= tree_parent[r, i] < i for i >= 1; tokens 1 to 7 have parent i - 1. accepted_path[r] lists, root first, the tokens on the path from token 0 to some token of request r's tree, then -1 entries; it holds 1 to 8 tokens, and 8 for some request. piece_owner[s] = (r, p) means slot s holds cache rows p * 256 to p * 256 + 255 of request r; (-1, -1) marks an unused slot. For each request r the pieces 0 to (cache_len[r] + 7) // 256 stand in exactly one slot each, and no other pieces do. cache_len[r] + 8 <= 1024.
All inputs are finite; a program needn't handle non-finite values.
Results may differ from the reference program's by a relative error of at most 0.02.
Values may be sent and summed in bfloat16 or wider, within the bound.
A program may use at most 64 MiB of HBM per device.

```python
import math
import jax
import jax.numpy as jnp
from jax import lax

D = 4096
H = 32
KVH = 8
HD = 128
TREE = 28
DEPTH = 8
PIECE = 256
MAXP = 4
REQS = 16
SLOTS = 48


def attention_inputs(key):
    base_key = jax.random.fold_in(key, 11)
    key_query, key_rows = jax.random.split(base_key, 2)
    query_vals = jax.random.truncated_normal(key_query, -4.0, 4.0, (REQS, TREE, H, HD), jnp.float32)
    tree_rows = jax.random.truncated_normal(key_rows, -4.0, 4.0, (REQS, TREE, KVH, 2, HD), jnp.float32)
    return (query_vals.reshape(REQS, TREE, H * HD), tree_rows.reshape(REQS, TREE, KVH * 2 * HD))


def tree_shape(key):
    base_key = jax.random.fold_in(key, 23)
    key_parent, key_pick, key_forced = jax.random.split(base_key, 3)
    node_ids = jnp.arange(TREE, dtype=jnp.int32)
    request_ids = jnp.arange(REQS, dtype=jnp.int32)
    forced = jax.random.randint(key_forced, (), 0, REQS)
    second = (forced + 1) % REQS
    raw_ints = jax.random.randint(key_parent, (REQS, TREE), 0, 1 << 20)
    parent = raw_ints % jnp.maximum(node_ids, 1)[None, :]
    parent = jnp.where(node_ids[None, :] < DEPTH, node_ids[None, :] - 1, parent).astype(jnp.int32)
    is_second = (request_ids == second)[:, None]
    parent = jnp.where(is_second & (node_ids[None, :] == TREE - 2), 0, parent)
    parent = jnp.where(is_second & (node_ids[None, :] == TREE - 1), TREE - 2, parent).astype(jnp.int32)
    depths = jnp.zeros((REQS, TREE), jnp.int32)
    for rounds in range(TREE):
        above = jnp.take_along_axis(depths, jnp.maximum(parent, 0), axis=1)
        depths = jnp.where(node_ids[None, :] > 0, above + 1, 0)
    scores = jax.random.randint(key_pick, (REQS, TREE), 0, 1 << 20) * TREE + node_ids[None, :]
    scores = jnp.where(depths < DEPTH, scores, -1)
    target = jnp.argmax(scores, axis=1).astype(jnp.int32)
    target = jnp.where(request_ids == forced, DEPTH - 1, target).astype(jnp.int32)
    target = jnp.where(request_ids == second, TREE - 1, target).astype(jnp.int32)
    target_depth = jnp.take_along_axis(depths, target[:, None], axis=1)[:, 0]
    path = jnp.full((REQS, DEPTH + 1), -1, jnp.int32)
    current = target
    for stepping in range(DEPTH):
        valid = stepping <= target_depth
        column = jnp.where(valid, target_depth - stepping, DEPTH)
        path = path.at[request_ids, column].set(jnp.where(valid, current, -1))
        upward = jnp.take_along_axis(parent, current[:, None], axis=1)[:, 0]
        current = jnp.where(current > 0, upward, 0).astype(jnp.int32)
    return (parent, path[:, :DEPTH])


def cache_layout(key):
    base_key = jax.random.fold_in(key, 37)
    key_count, key_pair, key_rest, key_forced, key_perm = jax.random.split(base_key, 5)
    half_reqs = REQS // 2
    order = jax.random.permutation(key_pair, REQS)
    first = jax.random.randint(key_count, (half_reqs,), 1, MAXP + 1)
    forced = jax.random.randint(key_forced, (), 0, half_reqs)
    first = jnp.where(jnp.arange(half_reqs) == forced, MAXP, first)
    paired = jnp.concatenate([first, MAXP + 1 - first]).astype(jnp.int32)
    pieces = jnp.zeros((REQS,), jnp.int32).at[order].set(paired)
    remainder = jax.random.randint(key_rest, (REQS,), 1, PIECE - DEPTH + 1)
    remainder = jnp.where(jnp.arange(REQS) == order[forced], PIECE - DEPTH, remainder)
    lengths = ((pieces - 1) * PIECE + remainder).astype(jnp.int32)
    ends = jnp.cumsum(pieces).astype(jnp.int32)
    starts = ends - pieces
    total = half_reqs * (MAXP + 1)
    global_ids = jnp.arange(SLOTS, dtype=jnp.int32)
    owner_req = jnp.sum((ends[None, :] <= global_ids[:, None]).astype(jnp.int32), axis=1)
    safe_req = jnp.minimum(owner_req, REQS - 1)
    owner_piece = global_ids - starts[safe_req]
    live = global_ids < total
    entries = jnp.stack([jnp.where(live, owner_req, -1), jnp.where(live, owner_piece, -1)], axis=1).astype(jnp.int32)
    shuffle = jax.random.permutation(key_perm, SLOTS)
    owners = jnp.full((SLOTS, 2), -1, jnp.int32).at[shuffle].set(entries)
    return (lengths, owners)


def draw_queries(key, part):
    return attention_inputs(key)[0].astype(jnp.bfloat16)


def draw_tree_kv(key, part):
    return attention_inputs(key)[1].astype(jnp.bfloat16)


def draw_tree_parent(key, part):
    return tree_shape(key)[0]


def draw_accepted_path(key, part):
    return tree_shape(key)[1]


def draw_cache_len(key, part):
    return cache_layout(key)[0]


def draw_piece_owner(key, part):
    return cache_layout(key)[1]


def level_of(key, dims, cuts, smallest, largest):
    level = 1.0
    for position, blocks in cuts:
        heights = jax.random.uniform(jax.random.fold_in(jax.random.fold_in(key, 6), position), (blocks,), jnp.float32, smallest / len(cuts), largest / len(cuts))
        level = level * jnp.repeat(jnp.exp(heights), dims[position] // blocks).reshape((-1,) + (1,) * (len(dims) - 1 - position))
    return level


def scatter_about(own_key, extent, scale, bound, cuts=(), held_as=jnp.bfloat16):
    values = scale * jax.random.normal(own_key, extent, jnp.float32)
    if cuts:
        values = values * level_of(own_key, extent, cuts, -0.22, 0.18)
    return jnp.clip(values, -bound, bound).astype(held_as)


def setup_inputs(seed: int = 0) -> dict:
    arg_keys = jax.random.split(jax.random.key(seed), 9)
    return {
        "queries": draw_queries(jax.random.fold_in(arg_keys[8], 71), 0),
        "tree_kv": draw_tree_kv(jax.random.fold_in(arg_keys[8], 71), 0),
        "tree_parent": draw_tree_parent(jax.random.fold_in(arg_keys[8], 71), 0),
        "accepted_path": draw_accepted_path(jax.random.fold_in(arg_keys[8], 71), 0),
        "cache_kv": scatter_about(arg_keys[4], (SLOTS, PIECE, KVH * 2 * HD), 1.0, 6.0, ((0, 16), (2, 2))),
        "piece_owner": draw_piece_owner(jax.random.fold_in(arg_keys[8], 71), 0),
        "cache_len": draw_cache_len(jax.random.fold_in(arg_keys[8], 71), 0),
        "out_weight": scatter_about(arg_keys[7], (H * HD, D), (H * HD) ** -0.5, 0.09375, ((0, 2), (1, 16))),
    }


NEG = -1e+30

def ancestors(parent):
    tree_size = parent.shape[-1]
    node_ids = lax.broadcasted_iota(jnp.int32, (tree_size, tree_size), 1)
    parent_hot = (parent[..., :, None] == node_ids).astype(jnp.float32)
    reached = jnp.minimum(parent_hot + jnp.eye(tree_size, dtype=jnp.float32), 1.0)
    for rounds in range(max(1, (tree_size - 1).bit_length())):
        reached = jnp.minimum(jnp.einsum('rij,rjk->rik', reached, reached, precision=lax.Precision.HIGHEST), 1.0)
    return reached

def reference(queries, tree_kv, tree_parent, accepted_path, cache_kv, piece_owner, cache_len, out_weight):
    group_size = H // KVH
    scaling = 1.0 / math.sqrt(HD)
    reached = ancestors(tree_parent)
    slot_ids = jnp.arange(SLOTS, dtype=jnp.int32)
    owner_req = piece_owner[:, 0]
    owner_piece = piece_owner[:, 1]
    flat_index = jnp.where(owner_req >= 0, owner_req * MAXP + owner_piece, REQS * MAXP).astype(jnp.int32)
    table = jnp.zeros((REQS * MAXP + 1,), jnp.int32).at[flat_index].set(slot_ids)
    table = table[:REQS * MAXP].reshape(REQS, MAXP)
    position_ids = jnp.arange(MAXP * PIECE, dtype=jnp.int32)

    def one_request(request):
        gathered = jnp.take(cache_kv, table[request], axis=0).reshape(MAXP * PIECE, KVH, 2, HD).astype(jnp.float32)
        visible = position_ids < cache_len[request]
        query = queries[request].reshape(TREE, KVH, group_size, HD).astype(jnp.float32)
        fresh = tree_kv[request].reshape(TREE, KVH, 2, HD).astype(jnp.float32)
        cache_scores = jnp.einsum('ikgd,tkd->ikgt', query, gathered[:, :, 0]) * scaling
        cache_scores = jnp.where(visible, cache_scores, NEG)
        tree_mask = reached[request][:, None, None, :] > 0.5
        tree_scores = jnp.where(tree_mask, jnp.einsum('ikgd,jkd->ikgj', query, fresh[:, :, 0]) * scaling, NEG)
        peak = jnp.maximum(lax.optimization_barrier(jnp.max(cache_scores, -1)), lax.optimization_barrier(jnp.max(tree_scores, -1)))
        cache_exp = jnp.where(visible, jnp.exp(cache_scores - peak[..., None]), 0.0)
        tree_exp = jnp.where(tree_mask, jnp.exp(tree_scores - peak[..., None]), 0.0)
        denom = lax.optimization_barrier(jnp.sum(cache_exp, -1)) + lax.optimization_barrier(jnp.sum(tree_exp, -1))
        cache_weights = lax.optimization_barrier(cache_exp.astype(jnp.bfloat16)).astype(jnp.float32)
        tree_weights = lax.optimization_barrier(tree_exp.astype(jnp.bfloat16)).astype(jnp.float32)
        numer = jnp.einsum('ikgt,tkd->ikgd', cache_weights, gathered[:, :, 1])
        numer = numer + jnp.einsum('ikgj,jkd->ikgd', tree_weights, fresh[:, :, 1])
        return (numer / denom[..., None]).reshape(TREE, H * HD).astype(jnp.bfloat16)
    attention = lax.map(one_request, jnp.arange(REQS, dtype=jnp.int32))
    mixed = jnp.dot(attention.reshape(REQS * TREE, H * HD), out_weight, preferred_element_type=jnp.float32)
    mixed = mixed.astype(jnp.bfloat16).reshape(REQS, TREE, D)
    columns = KVH * 2 * HD
    counts = lax.optimization_barrier(jnp.sum((accepted_path >= 0).astype(jnp.int32), axis=1))
    offsets = jnp.arange(DEPTH, dtype=jnp.int32)
    positions = cache_len[:, None] + offsets[None, :]
    slot_of = jnp.take_along_axis(table, (positions // PIECE).astype(jnp.int32), axis=1)
    valid = offsets[None, :] < counts[:, None]
    target = jnp.where(valid, slot_of * PIECE + positions % PIECE, SLOTS * PIECE).astype(jnp.int32)
    new_rows = jnp.take_along_axis(tree_kv, jnp.maximum(accepted_path, 0)[:, :, None].astype(jnp.int32), axis=1)
    flat_cache = cache_kv.reshape(SLOTS * PIECE, columns)
    flat_cache = flat_cache.at[target.reshape(-1)].set(new_rows.reshape(REQS * DEPTH, columns), mode='drop')
    cache_out = flat_cache.reshape(SLOTS, PIECE, columns)
    return (mixed, cache_out)
```

```python
import math

import jax
import jax.numpy as jnp
from jax import lax
from jax.experimental import pallas as pl
from jax.experimental.pallas import tpu as pltpu
from jax.sharding import PartitionSpec as P

HD = 128


NEG = -1e30


def ancestors(parent):
    tree_size = parent.shape[-1]
    node_ids = lax.broadcasted_iota(jnp.int32, (tree_size, tree_size), 1)
    parent_hot = (parent[..., :, None] == node_ids).astype(jnp.float32)
    reached = jnp.minimum(parent_hot + jnp.eye(tree_size, dtype=jnp.float32), 1.0)
    for rounds in range(max(1, (tree_size - 1).bit_length())):
        reached = jnp.minimum(
            jnp.einsum("rij,rjk->rik", reached, reached, precision=lax.Precision.HIGHEST), 1.0
        )
    return reached


def shards_general(
    queries, tree_kv, tree_parent, accepted_path, cache_kv, piece_owner, cache_len, out_weight
):
    kvheads_local = tree_kv.shape[-1] // (2 * HD)
    heads_local = queries.shape[-1] // HD
    group_size = heads_local // kvheads_local
    tree_size = queries.shape[1]
    slot_count = cache_kv.shape[0]
    piece_rows = cache_kv.shape[1]
    depth_most = accepted_path.shape[1]
    scaling = 1.0 / math.sqrt(HD)
    every_query = lax.all_gather(queries, "req", axis=0, tiled=True)
    req_total = every_query.shape[0]
    owner_req = piece_owner[:, 0]
    owner_piece = piece_owner[:, 1]
    safe_req = jnp.maximum(owner_req, 0)
    slot_query = every_query[safe_req].reshape(slot_count, tree_size, kvheads_local, group_size, HD)
    stored = cache_kv.reshape(slot_count, piece_rows, kvheads_local, 2, HD)
    row_pos = owner_piece[:, None] * piece_rows + lax.broadcasted_iota(
        jnp.int32, (slot_count, piece_rows), 1
    )
    visible = (owner_req >= 0)[:, None] & (row_pos < cache_len[safe_req][:, None])
    wide_mask = visible[:, None, None, None, :]
    scores = (
        jnp.einsum(
            "stkgd,spkd->stkgp", slot_query, stored[:, :, :, 0], preferred_element_type=jnp.float32
        )
        * scaling
    )
    scores = jnp.where(wide_mask, scores, NEG)
    slot_peak = jnp.max(scores, -1)
    expo = jnp.where(wide_mask, jnp.exp(scores - slot_peak[..., None]), 0.0)
    slot_den = jnp.sum(expo, -1)
    weights = expo.astype(jnp.bfloat16)
    slot_num = jnp.einsum(
        "stkgp,spkd->stkgd", weights, stored[:, :, :, 1], preferred_element_type=jnp.float32
    )
    request_ids = lax.broadcasted_iota(jnp.int32, (req_total, slot_count), 0)
    member = (owner_req[None, :] == request_ids)[:, :, None, None, None]
    req_peak = jnp.max(jnp.where(member, slot_peak[None], NEG), axis=1)
    factor = jnp.where(
        member, jnp.exp(jnp.where(member, slot_peak[None] - req_peak[:, None], 0.0)), 0.0
    )
    req_den = jnp.sum(factor * slot_den[None], axis=1)
    req_num = jnp.einsum("rstkg,stkgd->rtkgd", factor, slot_num, precision=lax.Precision.HIGHEST)
    peak_table = req_peak.reshape(req_total, tree_size, heads_local)
    den_table = req_den.reshape(req_total, tree_size, heads_local)
    num_table = req_num.reshape(req_total, tree_size, heads_local * HD)
    own_index = lax.axis_index("req")
    got_peak, got_den, got_num = (
        lax.all_to_all(
            peak_table.astype(jnp.bfloat16), "req", split_axis=0, concat_axis=0, tiled=True
        ).astype(peak_table.dtype),
        lax.all_to_all(
            den_table.astype(jnp.bfloat16), "req", split_axis=0, concat_axis=0, tiled=True
        ).astype(den_table.dtype),
        lax.all_to_all(
            num_table.astype(jnp.bfloat16), "req", split_axis=0, concat_axis=0, tiled=True
        ).astype(num_table.dtype),
    )
    cache_peak = jnp.max(got_peak, axis=0)
    source_scale = jnp.exp(got_peak - cache_peak[None])
    cache_den = jnp.sum(source_scale * got_den, axis=0)
    got_rows = got_num.reshape(got_num.shape[0], tree_size, heads_local, HD)
    cache_num = jnp.sum(source_scale[..., None] * got_rows, axis=0)
    reached = ancestors(tree_parent)[0]
    home_query = queries[0].reshape(tree_size, kvheads_local, group_size, HD)
    fresh = tree_kv[0].reshape(tree_size, kvheads_local, 2, HD)
    tree_mask = reached[:, None, None, :] > 0.5
    tree_scores = (
        jnp.einsum("ikgd,jkd->ikgj", home_query, fresh[:, :, 0], preferred_element_type=jnp.float32)
        * scaling
    )
    tree_scores = jnp.where(tree_mask, tree_scores, NEG)
    tree_peak = jnp.max(tree_scores, -1)
    tree_exp = jnp.where(tree_mask, jnp.exp(tree_scores - tree_peak[..., None]), 0.0)
    tree_den = jnp.sum(tree_exp, -1).reshape(tree_size, heads_local)
    tree_num = jnp.einsum(
        "ikgj,jkd->ikgd",
        tree_exp.astype(jnp.bfloat16),
        fresh[:, :, 1],
        preferred_element_type=jnp.float32,
    )
    tree_num = tree_num.reshape(tree_size, heads_local, HD)
    tree_peak = tree_peak.reshape(tree_size, heads_local)
    total_peak = jnp.maximum(cache_peak, tree_peak)
    cache_scale = jnp.exp(cache_peak - total_peak)
    tree_scale = jnp.exp(tree_peak - total_peak)
    denom = cache_den * cache_scale + tree_den * tree_scale
    numer = cache_num * cache_scale[..., None] + tree_num * tree_scale[..., None]
    attention = (
        (numer / denom[..., None]).reshape(1, tree_size, heads_local * HD).astype(jnp.bfloat16)
    )
    piece = lax.all_gather(attention, "req", axis=0, tiled=True)
    flat_rows = piece.reshape(piece.shape[0] * piece.shape[1], piece.shape[2])
    product = jnp.dot(flat_rows, out_weight, preferred_element_type=jnp.float32)
    terms = product.reshape(piece.shape[0], piece.shape[1], out_weight.shape[1])
    mixed = lax.psum_scatter(terms.astype(jnp.bfloat16), "tp", scatter_dimension=0, tiled=True)
    own_path = lax.dynamic_index_in_dim(accepted_path, own_index, 0, keepdims=False)
    picked = tree_kv[0][jnp.maximum(own_path, 0)]
    picked = jnp.where((own_path >= 0)[:, None], picked, jnp.zeros_like(picked))
    all_rows = lax.all_gather(picked[None], "req", axis=0, tiled=True)
    counts = jnp.sum((accepted_path >= 0).astype(jnp.int32), axis=1)
    offset = row_pos - cache_len[safe_req][:, None]
    writing = (owner_req >= 0)[:, None] & (offset >= 0) & (offset < counts[safe_req][:, None])
    slot_rows = all_rows[safe_req]
    chosen = jnp.take_along_axis(slot_rows, jnp.clip(offset, 0, depth_most - 1)[:, :, None], axis=1)
    cache_out = jnp.where(writing[:, :, None], chosen, cache_kv)
    return (mixed, cache_out)


MESH = pl.DeviceIdType.MESH
PAD = 32
KINDS = 19


def place():
    me = lax.axis_index("req")
    z, y, x = me // 4, (me // 2) % 2, me % 2
    planes = [z, z + 1 - 2 * (z % 2), (z + 2) % 4, 3 - z]
    return me, y, x, planes


class GridGather:
    def __init__(self, buf, send, recv):
        me, y, x, planes = place()
        self.buf, self.send, self.recv = buf, send, recv
        self.column = [plane * 4 + y * 2 + x for plane in planes]
        self.to_x, self.to_y = 1 - 2 * x, 2 - 4 * y
        self.me = me
        self.sent = []

    def copy(self, origin, part, target, kind):
        rows = self.buf.shape[1]
        half = rows // 2
        start, size = {"all": (0, rows), "top": (0, half), "low": (half, half)}[part]
        block = self.buf.at[origin, pl.ds(start, size)]
        return pltpu.make_async_remote_copy(
            src_ref=block,
            dst_ref=block,
            send_sem=self.send.at[kind],
            recv_sem=self.recv.at[kind],
            device_id={"req": target},
            device_id_type=MESH,
        )

    def go(self, *args):
        moving = self.copy(*args)
        moving.start()
        self.sent.append(moving)

    def run(self):
        me, column = self.me, self.column
        near_x, near_y = me + self.to_x, me + self.to_y
        for k in range(1, 4):
            self.go(me, "all", column[k], k - 1)
        for k in range(5):
            if k < 4:
                if k:
                    self.copy(column[k], "all", near_x, k - 1).wait_recv()
                self.go(column[k], "all", near_x, 3 + k)
                self.go(column[k], "all", near_y, 7 + k)
            if k:
                before = column[k - 1]
                self.copy(before + self.to_x, "all", near_x, 2 + k).wait_recv()
                self.go(before + self.to_x, "top", near_y, 10 + k)
                self.copy(before + self.to_y, "all", near_x, 6 + k).wait_recv()
                self.go(before + self.to_y, "low", near_x, 14 + k)
        for k in range(4):
            across = column[k] + self.to_x + self.to_y
            self.copy(across, "top", near_x, 11 + k).wait_recv()
            self.copy(across, "low", near_x, 15 + k).wait_recv()

    def finish(self):
        for moving in self.sent:
            moving.wait_send()


def iota(shape, dim):
    return lax.broadcasted_iota(jnp.int32, shape, dim)


def as_column(row):
    size = row.shape[1]
    shape = (size, size)
    return jnp.sum(
        jnp.where(iota(shape, 0) == iota(shape, 1), row, 0.0), axis=1, keepdims=True
    )


def attend(query, key, value, mask, scaling, owner):
    rows = query.shape[0]
    scores = scaling * lax.dot_general(
        query, key, (((1,), (1,)), ((), ())), preferred_element_type=jnp.float32
    )
    scores = jnp.where(mask, scores, NEG)
    peak = jnp.max(scores, axis=1, keepdims=True)
    expo = jnp.where(mask, jnp.exp(scores - peak), 0.0)
    denom = jnp.sum(expo, axis=1, keepdims=True)
    numer = jnp.dot(expo.astype(jnp.bfloat16), value, preferred_element_type=jnp.float32)
    some = denom > 0.0
    safe = jnp.where(some, denom, 1.0)
    level = jnp.where(some, peak + jnp.log(safe), NEG)
    out = numer * (1.0 / safe)
    shape = (PAD, HD)
    pick = iota(shape, 0) == iota(shape, 1)
    where = iota(shape, 0)
    blocks = []
    for g in range(rows // PAD):
        line = jnp.sum(
            jnp.where(pick, level[g * PAD : (g + 1) * PAD], 0.0), axis=0, keepdims=True
        )
        high = line.astype(jnp.bfloat16).astype(jnp.float32)
        block = out[g * PAD : (g + 1) * PAD]
        block = jnp.where(where == 28, high, block)
        block = jnp.where(where == 29, line - high, block)
        block = jnp.where(where == 30, owner, block)
        blocks.append(block.astype(jnp.bfloat16))
    return blocks


def layer_kernel(
    owner_ref, len_ref, parent_ref, path_ref, query_ref, tree_ref, cache_ref, weight_ref,
    mixed_ref, rows_ref,
    cache_v, weight_v, gathered, packed, tree_f, tree_b, reach_v, outgoing, incoming,
    wide, owners, joined, compact, attn, half_out, half_in,
    local_sem, send1, recv1, send2, recv2, send3, recv3, send4, recv4,
):
    me, y, x, planes = place()
    tp = lax.axis_index("tp")
    tree_size = query_ref.shape[1]
    slots = cache_ref.shape[0]
    piece_rows = cache_ref.shape[1]
    scaling = 1.0 / math.sqrt(HD)
    load_cache = pltpu.make_async_copy(cache_ref, cache_v, local_sem.at[0])
    load_weight = pltpu.make_async_copy(weight_ref, weight_v, local_sem.at[1])
    load_cache.start()
    load_weight.start()

    barrier = pltpu.get_barrier_semaphore()
    for d in range(1, 16):
        pl.semaphore_signal(
            barrier, inc=1, device_id={"req": (me + d) % 16}, device_id_type=MESH
        )
    pl.semaphore_signal(barrier, inc=1, device_id={"tp": 1 - tp}, device_id_type=MESH)

    tree_f[...] = jnp.zeros_like(tree_f)
    tree_f[0:tree_size] = tree_ref[0].astype(jnp.float32)
    tree_b[...] = tree_f[...].astype(jnp.bfloat16)
    path = as_column(path_ref[pl.ds(me, 1), :].astype(jnp.float32))
    depth = path.shape[0]
    chosen = (path == iota((depth, PAD), 1).astype(jnp.float32)).astype(jnp.bfloat16)
    picked = jnp.dot(chosen, tree_b[...], preferred_element_type=jnp.float32)
    width = tree_ref.shape[2]
    packed[0:tree_size] = query_ref[0].astype(jnp.float32)
    packed[tree_size:PAD, 0:width] = picked[0:4]
    packed[tree_size:PAD, width : 2 * width] = picked[4:8]
    gathered[me] = packed[...].astype(jnp.bfloat16)

    pl.semaphore_wait(barrier, 16)
    first = GridGather(gathered, send1, recv1)
    first.run()

    parent = as_column(parent_ref[...].astype(jnp.float32))
    lanes = iota((tree_size, PAD), 1).astype(jnp.float32)
    reach_v[...] = (iota((PAD, PAD), 0) == iota((PAD, PAD), 1)).astype(jnp.float32)
    reach_v[0:tree_size] = jnp.minimum(
        reach_v[0:tree_size] + (parent == lanes).astype(jnp.float32), 1.0
    )
    reached = reach_v[...]
    for rounds in range(max(1, (tree_size - 1).bit_length())):
        short = reached.astype(jnp.bfloat16)
        reached = jnp.minimum(jnp.dot(short, short, preferred_element_type=jnp.float32), 1.0)
    tree_mask = jnp.concatenate([reached] * 4, axis=0) > 0.5

    load_cache.wait()
    sent = []
    for k in range(4):
        plane = planes[k]
        for s in range(slots + 1):
            if s < slots:
                owner = owner_ref[s, 0]
                request = jnp.maximum(owner, 0)
                limit = jnp.where(owner >= 0, len_ref[request] - owner_ref[s, 1] * piece_rows, 0)
                mask = iota((4 * PAD, piece_rows), 1) < limit
                source, keys = request, cache_v.at[s]
                if k == 0:
                    rows_ref[s] = gathered[request, 16:32, :]
            else:
                owner, source, keys, mask = me, me, tree_b, tree_mask
            start = pl.multiple_of(plane * 4 * HD, 4 * HD)
            wide_q = gathered[source, :, pl.ds(start, 4 * HD)]
            query = jnp.concatenate([wide_q[:, g * HD : (g + 1) * HD] for g in range(4)], axis=0)
            at = pl.multiple_of(plane * 2 * HD, 2 * HD)
            both = keys[:, pl.ds(at, 2 * HD)]
            blocks = attend(
                query, both[:, :HD], both[:, HD:], mask, scaling, owner.astype(jnp.float32)
            )
            for g in range(4):
                outgoing[4 * k + g, s * PAD : (s + 1) * PAD] = blocks[g]
        for g in range(4):
            target = plane * 4 + g

            def remote(target=target, n=4 * k + g):
                return pltpu.make_async_remote_copy(
                    src_ref=outgoing.at[n],
                    dst_ref=incoming.at[me],
                    send_sem=send2.at[n],
                    recv_sem=recv2.at[me],
                    device_id={"req": target},
                    device_id_type=MESH,
                )

            if k == 0:

                @pl.when(target != me)
                def _():
                    remote().start()

                @pl.when(target == me)
                def _():
                    incoming[me] = outgoing[g]

            else:
                remote().start()
            sent.append((k, target, remote))
    for d in range(1, 16):
        source = (me + d) % 16
        pltpu.make_async_remote_copy(
            src_ref=outgoing.at[0],
            dst_ref=incoming.at[source],
            send_sem=send2.at[0],
            recv_sem=recv2.at[source],
            device_id={"req": source},
            device_id_type=MESH,
        ).wait_recv()

    pieces = 16 * (slots + 1)
    wide[...] = incoming[...].astype(jnp.float32).reshape(pieces * PAD, HD)
    level = wide[pl.ds(28, pieces, stride=PAD), :] + wide[pl.ds(29, pieces, stride=PAD), :]
    holder = wide[pl.ds(30, pieces, stride=PAD), :]
    owners[...] = holder
    share = jnp.zeros_like(level)
    for r in range(16):
        member = holder == float(r)
        peak = jnp.max(jnp.where(member, level, NEG), axis=0, keepdims=True)
        expo = jnp.where(member, jnp.exp(jnp.where(member, level - peak, 0.0)), 0.0)
        share = share + expo * (1.0 / jnp.sum(expo, axis=0, keepdims=True))
    turned = share.T
    for b in range(pieces):
        block = slice(b * PAD, (b + 1) * PAD)
        wide[block] = wide[block] * turned[0:PAD, b : b + 1]

    def join(r, carry):
        mine = r.astype(jnp.float32)
        first_row = pl.multiple_of((r * (slots + 1) + slots) * PAD, PAD)
        total = wide[pl.ds(first_row, PAD), :]
        for b in range(pieces):
            if b % (slots + 1) < slots:
                total = total + jnp.where(
                    owners[b : b + 1] == mine, wide[b * PAD : (b + 1) * PAD], 0.0
                )
        joined[r] = total
        return carry

    lax.fori_loop(0, 16, join, 0)
    for r in range(16):
        compact[r * tree_size : (r + 1) * tree_size] = joined[r, 0:tree_size]
    attn[me] = compact[...].astype(jnp.bfloat16)

    last = GridGather(attn, send3, recv3)
    last.run()
    load_weight.wait()
    size = half_out.shape[0]

    def project(part):
        begin = pl.multiple_of(part * size, size)
        total = jnp.zeros(half_out.shape, jnp.float32)
        for j in range(0, 16, 2):
            pair = jnp.concatenate(
                [attn[j, pl.ds(begin, size), :], attn[j + 1, pl.ds(begin, size), :]], axis=1
            )
            total = total + jnp.dot(
                pair, weight_v[j * HD : (j + 2) * HD], preferred_element_type=jnp.float32
            )
        return total

    half_out[...] = project(1 - tp).astype(jnp.bfloat16)
    swap = pltpu.make_async_remote_copy(
        src_ref=half_out,
        dst_ref=half_in,
        send_sem=send4,
        recv_sem=recv4,
        device_id={"tp": 1 - tp},
        device_id_type=MESH,
    )
    swap.start()
    own_half = project(tp)
    swap.wait_recv()
    mixed_ref[...] = (own_half + half_in[...].astype(jnp.float32)).astype(jnp.bfloat16)

    swap.wait_send()
    first.finish()
    last.finish()
    for k, target, remote in sent:
        if k == 0:

            @pl.when(target != me)
            def _():
                remote().wait_send()

        else:
            remote().wait_send()


def append_kernel(owner_ref, len_ref, path_ref, cache_ref, rows_ref, out_ref):
    s = pl.program_id(0)
    owner = owner_ref[s, 0]
    request = jnp.maximum(owner, 0)
    piece_rows, width = cache_ref.shape[1], cache_ref.shape[2]
    count = jnp.int32(0)
    for j in range(path_ref.shape[1]):
        count = count + (path_ref[request, j] >= 0).astype(jnp.int32)
    count = jnp.where(owner >= 0, count, 0)
    begin = len_ref[request] - owner_ref[s, 1] * piece_rows
    offset = iota((piece_rows, 16), 0) - begin
    lane = iota((piece_rows, 16), 1) - 12
    low = ((offset == lane) & (lane >= 0)).astype(jnp.bfloat16)
    high = ((offset == lane + 4) & (lane >= 0)).astype(jnp.bfloat16)
    rows = rows_ref[0]
    chosen = jnp.dot(low, rows[:, :width], preferred_element_type=jnp.float32) + jnp.dot(
        high, rows[:, width:], preferred_element_type=jnp.float32
    )
    offset = iota((piece_rows, width), 0) - begin
    writing = (offset >= 0) & (offset < count)
    out_ref[0] = jnp.where(writing, chosen, cache_ref[0].astype(jnp.float32)).astype(jnp.bfloat16)


def shards_grid(
    queries, tree_kv, tree_parent, accepted_path, cache_kv, piece_owner, cache_len, out_weight
):
    slots, piece_rows, width = cache_kv.shape
    tree_size = queries.shape[1]
    columns = queries.shape[2]
    reqs = 16
    half = reqs * tree_size // 2
    smem = pl.BlockSpec(memory_space=pltpu.SMEM)
    vmem = pl.BlockSpec(memory_space=pltpu.VMEM)
    anywhere = pl.BlockSpec(memory_space=pl.ANY)
    pieces = reqs * (slots + 1)
    dma = pltpu.SemaphoreType.DMA
    bf16, f32 = jnp.bfloat16, jnp.float32
    mixed, rows = pl.pallas_call(
        layer_kernel,
        out_shape=(
            jax.ShapeDtypeStruct((half, out_weight.shape[1]), bf16),
            jax.ShapeDtypeStruct((slots, 16, columns), bf16),
        ),
        in_specs=[smem, smem, vmem, vmem, vmem, vmem, anywhere, anywhere],
        out_specs=(vmem, vmem),
        scratch_shapes=[
            pltpu.VMEM(cache_kv.shape, bf16),
            pltpu.VMEM(out_weight.shape, bf16),
            pltpu.VMEM((reqs, PAD, columns), bf16),
            pltpu.VMEM((PAD, columns), f32),
            pltpu.VMEM((PAD, width), f32),
            pltpu.VMEM((PAD, width), bf16),
            pltpu.VMEM((PAD, PAD), f32),
            pltpu.VMEM((reqs, (slots + 1) * PAD, HD), bf16),
            pltpu.VMEM((reqs, (slots + 1) * PAD, HD), bf16),
            pltpu.VMEM((pieces * PAD, HD), f32),
            pltpu.VMEM((pieces, HD), f32),
            pltpu.VMEM((reqs, PAD, HD), f32),
            pltpu.VMEM((reqs * tree_size, HD), f32),
            pltpu.VMEM((reqs, reqs * tree_size, HD), bf16),
            pltpu.VMEM((half, out_weight.shape[1]), bf16),
            pltpu.VMEM((half, out_weight.shape[1]), bf16),
            dma((2,)),
            dma((KINDS,)),
            dma((KINDS,)),
            dma((reqs,)),
            dma((reqs,)),
            dma((KINDS,)),
            dma((KINDS,)),
            dma,
            dma,
        ],
        compiler_params=pltpu.CompilerParams(
            collective_id=0, has_side_effects=True, vmem_limit_bytes=48 * 1024 * 1024
        ),
    )(
        piece_owner, cache_len, tree_parent, accepted_path, queries, tree_kv, cache_kv, out_weight
    )
    block = pl.BlockSpec((1, piece_rows, width), lambda s: (s, 0, 0))
    cache_out = pl.pallas_call(
        append_kernel,
        out_shape=jax.ShapeDtypeStruct(cache_kv.shape, bf16),
        grid=(slots,),
        in_specs=[smem, smem, smem, block, pl.BlockSpec((1, 16, columns), lambda s: (s, 0, 0))],
        out_specs=block,
        compiler_params=pltpu.CompilerParams(vmem_limit_bytes=32 * 1024 * 1024),
    )(piece_owner, cache_len, accepted_path, cache_kv, rows)
    return mixed.reshape(reqs // 2, tree_size, out_weight.shape[1]), cache_out


def solution(mesh):
    body = shards_grid if dict(mesh.shape) == {"req": 16, "tp": 2} else shards_general
    return jax.shard_map(
        body,
        mesh=mesh,
        in_specs=(
            P("req", None, "tp"),
            P("req", None, "tp"),
            P("req", None),
            P(),
            P("req", None, "tp"),
            P("req", None),
            P(),
            P("tp", "req"),
        ),
        out_specs=(P("tp", None, "req"), P("req", None, "tp")),
        check_vma=False,
    )
```

```python
import math

import jax
import jax.numpy as jnp
from jax import lax
from jax.experimental import pallas as pl
from jax.experimental.pallas import tpu as pltpu
from jax.sharding import PartitionSpec as P

HD = 128


NEG = -1e30


def ancestors(parent):
    tree_size = parent.shape[-1]
    node_ids = lax.broadcasted_iota(jnp.int32, (tree_size, tree_size), 1)
    parent_hot = (parent[..., :, None] == node_ids).astype(jnp.float32)
    reached = jnp.minimum(parent_hot + jnp.eye(tree_size, dtype=jnp.float32), 1.0)
    for rounds in range(max(1, (tree_size - 1).bit_length())):
        reached = jnp.minimum(
            jnp.einsum("rij,rjk->rik", reached, reached, precision=lax.Precision.HIGHEST), 1.0
        )
    return reached


def shards_general(
    queries, tree_kv, tree_parent, accepted_path, cache_kv, piece_owner, cache_len, out_weight
):
    kvheads_local = tree_kv.shape[-1] // (2 * HD)
    heads_local = queries.shape[-1] // HD
    group_size = heads_local // kvheads_local
    tree_size = queries.shape[1]
    slot_count = cache_kv.shape[0]
    piece_rows = cache_kv.shape[1]
    depth_most = accepted_path.shape[1]
    scaling = 1.0 / math.sqrt(HD)
    every_query = lax.all_gather(queries, "req", axis=0, tiled=True)
    req_total = every_query.shape[0]
    owner_req = piece_owner[:, 0]
    owner_piece = piece_owner[:, 1]
    safe_req = jnp.maximum(owner_req, 0)
    slot_query = every_query[safe_req].reshape(slot_count, tree_size, kvheads_local, group_size, HD)
    stored = cache_kv.reshape(slot_count, piece_rows, kvheads_local, 2, HD)
    row_pos = owner_piece[:, None] * piece_rows + lax.broadcasted_iota(
        jnp.int32, (slot_count, piece_rows), 1
    )
    visible = (owner_req >= 0)[:, None] & (row_pos < cache_len[safe_req][:, None])
    wide_mask = visible[:, None, None, None, :]
    scores = (
        jnp.einsum(
            "stkgd,spkd->stkgp", slot_query, stored[:, :, :, 0], preferred_element_type=jnp.float32
        )
        * scaling
    )
    scores = jnp.where(wide_mask, scores, NEG)
    slot_peak = jnp.max(scores, -1)
    expo = jnp.where(wide_mask, jnp.exp(scores - slot_peak[..., None]), 0.0)
    slot_den = jnp.sum(expo, -1)
    weights = expo.astype(jnp.bfloat16)
    slot_num = jnp.einsum(
        "stkgp,spkd->stkgd", weights, stored[:, :, :, 1], preferred_element_type=jnp.float32
    )
    request_ids = lax.broadcasted_iota(jnp.int32, (req_total, slot_count), 0)
    member = (owner_req[None, :] == request_ids)[:, :, None, None, None]
    req_peak = jnp.max(jnp.where(member, slot_peak[None], NEG), axis=1)
    factor = jnp.where(
        member, jnp.exp(jnp.where(member, slot_peak[None] - req_peak[:, None], 0.0)), 0.0
    )
    req_den = jnp.sum(factor * slot_den[None], axis=1)
    req_num = jnp.einsum("rstkg,stkgd->rtkgd", factor, slot_num, precision=lax.Precision.HIGHEST)
    peak_table = req_peak.reshape(req_total, tree_size, heads_local)
    den_table = req_den.reshape(req_total, tree_size, heads_local)
    num_table = req_num.reshape(req_total, tree_size, heads_local * HD)
    own_index = lax.axis_index("req")
    got_peak, got_den, got_num = (
        lax.all_to_all(
            peak_table.astype(jnp.bfloat16), "req", split_axis=0, concat_axis=0, tiled=True
        ).astype(peak_table.dtype),
        lax.all_to_all(
            den_table.astype(jnp.bfloat16), "req", split_axis=0, concat_axis=0, tiled=True
        ).astype(den_table.dtype),
        lax.all_to_all(
            num_table.astype(jnp.bfloat16), "req", split_axis=0, concat_axis=0, tiled=True
        ).astype(num_table.dtype),
    )
    cache_peak = jnp.max(got_peak, axis=0)
    source_scale = jnp.exp(got_peak - cache_peak[None])
    cache_den = jnp.sum(source_scale * got_den, axis=0)
    got_rows = got_num.reshape(got_num.shape[0], tree_size, heads_local, HD)
    cache_num = jnp.sum(source_scale[..., None] * got_rows, axis=0)
    reached = ancestors(tree_parent)[0]
    home_query = queries[0].reshape(tree_size, kvheads_local, group_size, HD)
    fresh = tree_kv[0].reshape(tree_size, kvheads_local, 2, HD)
    tree_mask = reached[:, None, None, :] > 0.5
    tree_scores = (
        jnp.einsum("ikgd,jkd->ikgj", home_query, fresh[:, :, 0], preferred_element_type=jnp.float32)
        * scaling
    )
    tree_scores = jnp.where(tree_mask, tree_scores, NEG)
    tree_peak = jnp.max(tree_scores, -1)
    tree_exp = jnp.where(tree_mask, jnp.exp(tree_scores - tree_peak[..., None]), 0.0)
    tree_den = jnp.sum(tree_exp, -1).reshape(tree_size, heads_local)
    tree_num = jnp.einsum(
        "ikgj,jkd->ikgd",
        tree_exp.astype(jnp.bfloat16),
        fresh[:, :, 1],
        preferred_element_type=jnp.float32,
    )
    tree_num = tree_num.reshape(tree_size, heads_local, HD)
    tree_peak = tree_peak.reshape(tree_size, heads_local)
    total_peak = jnp.maximum(cache_peak, tree_peak)
    cache_scale = jnp.exp(cache_peak - total_peak)
    tree_scale = jnp.exp(tree_peak - total_peak)
    denom = cache_den * cache_scale + tree_den * tree_scale
    numer = cache_num * cache_scale[..., None] + tree_num * tree_scale[..., None]
    attention = (
        (numer / denom[..., None]).reshape(1, tree_size, heads_local * HD).astype(jnp.bfloat16)
    )
    piece = lax.all_gather(attention, "req", axis=0, tiled=True)
    flat_rows = piece.reshape(piece.shape[0] * piece.shape[1], piece.shape[2])
    product = jnp.dot(flat_rows, out_weight, preferred_element_type=jnp.float32)
    terms = product.reshape(piece.shape[0], piece.shape[1], out_weight.shape[1])
    mixed = lax.psum_scatter(terms.astype(jnp.bfloat16), "tp", scatter_dimension=0, tiled=True)
    own_path = lax.dynamic_index_in_dim(accepted_path, own_index, 0, keepdims=False)
    picked = tree_kv[0][jnp.maximum(own_path, 0)]
    picked = jnp.where((own_path >= 0)[:, None], picked, jnp.zeros_like(picked))
    all_rows = lax.all_gather(picked[None], "req", axis=0, tiled=True)
    counts = jnp.sum((accepted_path >= 0).astype(jnp.int32), axis=1)
    offset = row_pos - cache_len[safe_req][:, None]
    writing = (owner_req >= 0)[:, None] & (offset >= 0) & (offset < counts[safe_req][:, None])
    slot_rows = all_rows[safe_req]
    chosen = jnp.take_along_axis(slot_rows, jnp.clip(offset, 0, depth_most - 1)[:, :, None], axis=1)
    cache_out = jnp.where(writing[:, :, None], chosen, cache_kv)
    return (mixed, cache_out)


MESH = pl.DeviceIdType.MESH
PAD = 32
KINDS = 19
VMEM_LIMIT = 63 * 1024 * 1024


def place():
    me = lax.axis_index("req")
    z, y, x = me // 4, (me // 2) % 2, me % 2
    planes = [z, z + 1 - 2 * (z % 2), (z + 2) % 4, 3 - z]
    return me, y, x, planes


class GridGather:
    def __init__(self, buf, send, recv, part):
        me, y, x, planes = place()
        self.buf, self.send, self.recv, self.part = buf, send, recv, part
        self.column = [plane * 4 + y * 2 + x for plane in planes]
        self.to_x, self.to_y = 1 - 2 * x, 2 - 4 * y
        self.near_x, self.near_y = me + self.to_x, me + self.to_y
        self.me = me
        self.sent = []

    def copy(self, origin, piece, target, kind):
        rows = self.buf.shape[1]
        half = rows // 2
        start, size = {"all": (0, rows), "top": (0, half), "low": (half, half)}[piece]
        block = self.buf.at[origin, pl.ds(start, size)]
        return pltpu.make_async_remote_copy(
            src_ref=block,
            dst_ref=block,
            send_sem=self.send.at[self.part, kind],
            recv_sem=self.recv.at[self.part, kind],
            device_id={"req": target},
            device_id_type=MESH,
        )

    def go(self, *args):
        moving = self.copy(*args)
        moving.start()
        self.sent.append(moving)

    def begin(self):
        for k in range(1, 4):
            self.go(self.me, "all", self.column[k], k - 1)
        self.step(0)

    def step(self, k):
        column = self.column
        if k < 4:
            if k:
                self.copy(column[k], "all", self.near_x, k - 1).wait_recv()
            self.go(column[k], "all", self.near_x, 3 + k)
            self.go(column[k], "all", self.near_y, 7 + k)
        if k:
            across_x, across_y = column[k - 1] + self.to_x, column[k - 1] + self.to_y
            self.copy(across_x, "all", self.near_x, 2 + k).wait_recv()
            self.go(across_x, "top", self.near_y, 10 + k)
            self.copy(across_y, "all", self.near_x, 6 + k).wait_recv()
            self.go(across_y, "low", self.near_x, 14 + k)

    def end(self):
        for k in range(4):
            across = self.column[k] + self.to_x + self.to_y
            self.copy(across, "top", self.near_x, 11 + k).wait_recv()
            self.copy(across, "low", self.near_x, 15 + k).wait_recv()

    def finish(self):
        for moving in self.sent:
            moving.wait_send()


def iota(shape, dim):
    return lax.broadcasted_iota(jnp.int32, shape, dim)


def as_column(row):
    size = row.shape[1]
    shape = (size, size)
    return jnp.sum(
        jnp.where(iota(shape, 0) == iota(shape, 1), row, 0.0), axis=1, keepdims=True
    )


def attend(query, key, value, mask, scaling, owner):
    rows = query.shape[0]
    scores = scaling * lax.dot_general(
        query, key, (((1,), (1,)), ((), ())), preferred_element_type=jnp.float32
    )
    scores = jnp.where(mask, scores, NEG)
    peak = jnp.max(scores, axis=1, keepdims=True)
    expo = jnp.where(mask, jnp.exp(scores - peak), 0.0)
    denom = jnp.sum(expo, axis=1, keepdims=True)
    numer = jnp.dot(expo.astype(jnp.bfloat16), value, preferred_element_type=jnp.float32)
    some = denom > 0.0
    safe = jnp.where(some, denom, 1.0)
    level = jnp.where(some, peak + jnp.log(safe), NEG)
    out = numer * (1.0 / safe)
    shape = (PAD, HD)
    pick = iota(shape, 0) == iota(shape, 1)
    where = iota(shape, 0)
    blocks = []
    for g in range(rows // PAD):
        line = jnp.sum(
            jnp.where(pick, level[g * PAD : (g + 1) * PAD], 0.0), axis=0, keepdims=True
        )
        high = line.astype(jnp.bfloat16).astype(jnp.float32)
        block = out[g * PAD : (g + 1) * PAD]
        block = jnp.where(where == 28, high, block)
        block = jnp.where(where == 29, line - high, block)
        block = jnp.where(where == 30, owner, block)
        blocks.append(block.astype(jnp.bfloat16))
    return blocks


def layer_kernel(
    owner_h, len_h, parent_h, path_h, query_h, tree_h, cache_h, weight_h,
    mixed_ref, rows_ref,
    owner_ref, len_ref, parent_ref, path_ref, query_ref, tree_ref, cache_v, weight_v,
    gathered_a, gathered_b, packed, tree_f, tree_b, reach_v, outgoing, incoming,
    wide, owners, joined, compact, attn, half_out, half_in,
    local_sem, send1, recv1, send2, recv2, send3, recv3, send4, recv4,
):
    me, y, x, planes = place()
    tp = lax.axis_index("tp")
    gathered = [gathered_a, gathered_b]
    tree_size = query_h.shape[1]
    slots = cache_h.shape[0]
    piece_rows = cache_h.shape[1]
    scaling = 1.0 / math.sqrt(HD)
    pairs = [
        (query_h, query_ref), (tree_h, tree_ref), (path_h, path_ref), (parent_h, parent_ref),
        (owner_h, owner_ref), (len_h, len_ref), (cache_h, cache_v), (weight_h, weight_v),
    ]
    loads = [
        pltpu.make_async_copy(there, here, local_sem.at[n])
        for n, (there, here) in enumerate(pairs)
    ]
    for load in loads:
        load.start()

    barrier = pltpu.get_barrier_semaphore()
    for d in range(1, 16):
        pl.semaphore_signal(
            barrier, inc=1, device_id={"req": (me + d) % 16}, device_id_type=MESH
        )
    pl.semaphore_signal(barrier, inc=1, device_id={"tp": 1 - tp}, device_id_type=MESH)

    for load in loads[:3]:
        load.wait()
    tree_f[...] = jnp.zeros_like(tree_f)
    tree_f[0:tree_size] = tree_ref[0].astype(jnp.float32)
    tree_b[...] = tree_f[...].astype(jnp.bfloat16)
    table = path_ref[...].astype(jnp.float32)
    path = jnp.sum(jnp.where(iota(table.shape, 1) == me, table, 0.0), axis=1, keepdims=True)
    depth = path.shape[0]
    chosen = (path == iota((depth, PAD), 1).astype(jnp.float32)).astype(jnp.bfloat16)
    picked = jnp.dot(chosen, tree_b[...], preferred_element_type=jnp.float32)
    width = tree_h.shape[2]
    packed[0:tree_size] = query_ref[0].astype(jnp.float32)
    packed[tree_size:PAD, 0:width] = picked[0:4]
    packed[tree_size:PAD, width : 2 * width] = picked[4:8]
    for c in range(2):
        gathered[c][me] = packed[:, c * width : (c + 1) * width].astype(jnp.bfloat16)

    pl.semaphore_wait(barrier, 16)
    first = [GridGather(gathered[c], send1, recv1, c) for c in range(2)]
    first[0].begin()
    first[0].step(1)
    first[1].begin()
    first[0].step(2)
    first[0].step(3)
    first[1].step(1)

    loads[3].wait()
    parent = as_column(parent_ref[...].astype(jnp.float32))
    lanes = iota((tree_size, PAD), 1).astype(jnp.float32)
    reach_v[...] = (iota((PAD, PAD), 0) == iota((PAD, PAD), 1)).astype(jnp.float32)
    reach_v[0:tree_size] = jnp.minimum(
        reach_v[0:tree_size] + (parent == lanes).astype(jnp.float32), 1.0
    )
    reached = reach_v[...]
    for rounds in range(max(1, (tree_size - 1).bit_length())):
        short = reached.astype(jnp.bfloat16)
        reached = jnp.minimum(jnp.dot(short, short, preferred_element_type=jnp.float32), 1.0)
    tree_mask = jnp.concatenate([reached] * 4, axis=0) > 0.5
    first[0].step(4)
    first[1].step(2)
    for load in loads[4:7]:
        load.wait()

    sent = []

    def attend_head(kv):
        c, offset = kv // 2, (kv % 2) * 4 * HD
        for s in range(slots + 1):
            if s < slots:
                owner = owner_ref[0, s]
                request = jnp.maximum(owner, 0)
                limit = jnp.where(owner >= 0, len_ref[request] - owner_ref[1, s] * piece_rows, 0)
                mask = iota((4 * PAD, piece_rows), 1) < limit
                source, keys = request, cache_v.at[s]
            else:
                owner, source, keys, mask = me, me, tree_b, tree_mask
            wide_q = gathered[c][source, :, offset : offset + 4 * HD]
            query = jnp.concatenate([wide_q[:, g * HD : (g + 1) * HD] for g in range(4)], axis=0)
            at = kv * 2 * HD
            blocks = attend(
                query, keys[:, at : at + HD], keys[:, at + HD : at + 2 * HD], mask, scaling,
                owner.astype(jnp.float32),
            )
            for g in range(4):
                outgoing[kv, g, s * PAD : (s + 1) * PAD] = blocks[g]
        for k in range(4):
            plane = planes[k]
            target = plane * 4 + kv

            def remote(target=target, plane=plane, k=k):
                return pltpu.make_async_remote_copy(
                    src_ref=outgoing.at[kv, plane],
                    dst_ref=incoming.at[me],
                    send_sem=send2.at[kv, k],
                    recv_sem=recv2.at[me],
                    device_id={"req": target},
                    device_id_type=MESH,
                )

            if k == 0:

                @pl.when(target != me)
                def _():
                    remote().start()

                @pl.when(target == me)
                def _():
                    incoming[me] = outgoing[kv, plane]

            else:
                remote().start()
            sent.append((k, target, remote))

    first[0].end()
    attend_head(0)
    first[1].step(3)
    attend_head(1)
    first[1].step(4)
    first[1].end()
    attend_head(2)
    attend_head(3)
    for s in range(slots):
        request = jnp.maximum(owner_ref[0, s], 0)
        for c in range(2):
            rows_ref[s, :, c * width : (c + 1) * width] = gathered[c][request, 16:32, :]
    for d in range(1, 16):
        source = (me + d) % 16
        pltpu.make_async_remote_copy(
            src_ref=outgoing.at[0, 0],
            dst_ref=incoming.at[source],
            send_sem=send2.at[0, 0],
            recv_sem=recv2.at[source],
            device_id={"req": source},
            device_id_type=MESH,
        ).wait_recv()

    pieces = 16 * (slots + 1)
    wide[...] = incoming[...].astype(jnp.float32).reshape(pieces * PAD, HD)
    level = wide[pl.ds(28, pieces, stride=PAD), :] + wide[pl.ds(29, pieces, stride=PAD), :]
    holder = wide[pl.ds(30, pieces, stride=PAD), :]
    owners[...] = holder
    share = jnp.zeros_like(level)
    for r in range(16):
        member = holder == float(r)
        peak = jnp.max(jnp.where(member, level, NEG), axis=0, keepdims=True)
        expo = jnp.where(member, jnp.exp(jnp.where(member, level - peak, 0.0)), 0.0)
        share = share + expo * (1.0 / jnp.sum(expo, axis=0, keepdims=True))
    turned = share.T
    for b in range(pieces):
        block = slice(b * PAD, (b + 1) * PAD)
        wide[block] = wide[block] * turned[0:PAD, b : b + 1]

    def join_half(part, to):
        def join(i, carry):
            r = part * 8 + i
            mine = r.astype(jnp.float32)
            first_row = pl.multiple_of((r * (slots + 1) + slots) * PAD, PAD)
            total = wide[pl.ds(first_row, PAD), :]
            for b in range(pieces):
                if b % (slots + 1) < slots:
                    total = total + jnp.where(
                        owners[b : b + 1] == mine, wide[b * PAD : (b + 1) * PAD], 0.0
                    )
            joined[i] = total
            return carry

        lax.fori_loop(0, 8, join, 0)
        for i in range(8):
            compact[pl.ds(i, tree_size, stride=8), :] = joined[i, 0:tree_size]
        attn[to, me] = compact[...].astype(jnp.bfloat16)

    last = [GridGather(attn.at[c], send3, recv3, c) for c in range(2)]
    join_half(1 - tp, 0)
    last[0].begin()
    join_half(tp, 1)
    last[0].step(1)
    last[1].begin()
    last[0].step(2)
    last[1].step(1)
    last[0].step(3)
    last[1].step(2)
    last[0].step(4)
    last[1].step(3)
    loads[7].wait()

    def project(part):
        total = jnp.zeros(half_out.shape, jnp.float32)
        for kv in range(4):
            for g in range(0, 4, 2):
                head = 4 * kv + g
                pair = jnp.concatenate(
                    [attn[part, 4 * g + kv], attn[part, 4 * g + 4 + kv]], axis=1
                )
                total = total + jnp.dot(
                    pair, weight_v[head * HD : (head + 2) * HD],
                    preferred_element_type=jnp.float32,
                )
        return total

    last[0].end()
    last[1].step(4)
    half_out[...] = project(0).astype(jnp.bfloat16)
    swap = pltpu.make_async_remote_copy(
        src_ref=half_out,
        dst_ref=half_in,
        send_sem=send4,
        recv_sem=recv4,
        device_id={"tp": 1 - tp},
        device_id_type=MESH,
    )
    swap.start()
    last[1].end()
    own_half = project(1)
    swap.wait_recv()
    mixed_ref[...] = (own_half + half_in[...].astype(jnp.float32)).astype(jnp.bfloat16)

    swap.wait_send()
    for gather in first + last:
        gather.finish()
    for k, target, remote in sent:
        if k == 0:

            @pl.when(target != me)
            def _():
                remote().wait_send()

        else:
            remote().wait_send()


def append_kernel(owner_ref, len_ref, path_ref, cache_ref, rows_ref, out_ref, sems, *held):
    slots, piece_rows, width = cache_ref.shape
    span = 32
    loads = [pltpu.make_async_copy(cache_ref.at[s], held[s], sems.at[s]) for s in range(slots)]
    stores = [
        pltpu.make_async_copy(held[s], out_ref.at[s], sems.at[slots + s]) for s in range(slots)
    ]
    for load in loads:
        load.start()
    for s in range(slots):
        request = jnp.maximum(owner_ref[0, s], 0)
        begin = len_ref[request] - owner_ref[1, s] * piece_rows
        start = pl.multiple_of(jnp.clip(begin, 0, piece_rows - span) // 16 * 16, 16)
        count = jnp.int32(0)
        for j in range(path_ref.shape[0]):
            count = count + (path_ref[j, request] >= 0).astype(jnp.int32)
        count = jnp.where(owner_ref[0, s] >= 0, count, 0)
        offset = iota((span, 16), 0) + (start - begin)
        lane = iota((span, 16), 1) - 12
        low = ((offset == lane) & (lane >= 0)).astype(jnp.bfloat16)
        high = ((offset == lane + 4) & (lane >= 0)).astype(jnp.bfloat16)
        chosen = jnp.dot(
            low, rows_ref[s, :, :width], preferred_element_type=jnp.float32
        ) + jnp.dot(high, rows_ref[s, :, width:], preferred_element_type=jnp.float32)
        offset = iota((span, width), 0) + (start - begin)
        writing = (offset >= 0) & (offset < count)
        loads[s].wait()
        near = held[s][pl.ds(start, span), :].astype(jnp.float32)
        held[s][pl.ds(start, span), :] = jnp.where(writing, chosen, near).astype(jnp.bfloat16)
        stores[s].start()
    for store in stores:
        store.wait()


def shards_grid(
    queries, tree_kv, tree_parent, accepted_path, cache_kv, piece_owner, cache_len, out_weight
):
    slots, piece_rows, width = cache_kv.shape
    tree_size = queries.shape[1]
    columns = queries.shape[2]
    reqs = 16
    half = reqs * tree_size // 2
    smem = pl.BlockSpec(memory_space=pltpu.SMEM)
    vmem = pl.BlockSpec(memory_space=pltpu.VMEM)
    hbm = pl.BlockSpec(memory_space=pltpu.HBM)
    pieces = reqs * (slots + 1)
    dma = pltpu.SemaphoreType.DMA
    bf16, f32, i32 = jnp.bfloat16, jnp.float32, jnp.int32
    owner_t, path_t = piece_owner.T, accepted_path.T
    mixed, rows = pl.pallas_call(
        layer_kernel,
        out_shape=(
            jax.ShapeDtypeStruct((half, out_weight.shape[1]), bf16),
            jax.ShapeDtypeStruct((slots, 16, columns), bf16),
        ),
        in_specs=[hbm] * 8,
        out_specs=(vmem, vmem),
        scratch_shapes=[
            pltpu.SMEM(owner_t.shape, i32),
            pltpu.SMEM(cache_len.shape, i32),
            pltpu.VMEM(tree_parent.shape, i32),
            pltpu.VMEM(path_t.shape, i32),
            pltpu.VMEM(queries.shape, bf16),
            pltpu.VMEM(tree_kv.shape, bf16),
            pltpu.VMEM(cache_kv.shape, bf16),
            pltpu.VMEM(out_weight.shape, bf16),
            pltpu.VMEM((reqs, PAD, columns // 2), bf16),
            pltpu.VMEM((reqs, PAD, columns // 2), bf16),
            pltpu.VMEM((PAD, columns), f32),
            pltpu.VMEM((PAD, width), f32),
            pltpu.VMEM((PAD, width), bf16),
            pltpu.VMEM((PAD, PAD), f32),
            pltpu.VMEM((4, 4, (slots + 1) * PAD, HD), bf16),
            pltpu.VMEM((reqs, (slots + 1) * PAD, HD), bf16),
            pltpu.VMEM((pieces * PAD, HD), f32),
            pltpu.VMEM((pieces, HD), f32),
            pltpu.VMEM((reqs // 2, PAD, HD), f32),
            pltpu.VMEM((half, HD), f32),
            pltpu.VMEM((2, reqs, half, HD), bf16),
            pltpu.VMEM((half, out_weight.shape[1]), bf16),
            pltpu.VMEM((half, out_weight.shape[1]), bf16),
            dma((8,)),
            dma((2, KINDS)),
            dma((2, KINDS)),
            dma((4, 4)),
            dma((reqs,)),
            dma((2, KINDS)),
            dma((2, KINDS)),
            dma,
            dma,
        ],
        compiler_params=pltpu.CompilerParams(
            collective_id=0, has_side_effects=True, vmem_limit_bytes=VMEM_LIMIT
        ),
    )(owner_t, cache_len, tree_parent, path_t, queries, tree_kv, cache_kv, out_weight)
    cache_out = pl.pallas_call(
        append_kernel,
        out_shape=jax.ShapeDtypeStruct(cache_kv.shape, bf16),
        in_specs=[smem, smem, smem, hbm, vmem],
        out_specs=hbm,
        scratch_shapes=[dma((2 * slots,))] + [pltpu.VMEM(cache_kv.shape[1:], bf16)] * slots,
        compiler_params=pltpu.CompilerParams(vmem_limit_bytes=VMEM_LIMIT),
    )(owner_t, cache_len, path_t, cache_kv, rows)
    mixed = mixed.reshape(tree_size, reqs // 2, out_weight.shape[1]).transpose(1, 0, 2)
    return mixed, cache_out


def solution(mesh):
    body = shards_grid if dict(mesh.shape) == {"req": 16, "tp": 2} else shards_general
    return jax.shard_map(
        body,
        mesh=mesh,
        in_specs=(
            P("req", None, "tp"),
            P("req", None, "tp"),
            P("req", None),
            P(),
            P("req", None, "tp"),
            P("req", None),
            P(),
            P("tp", "req"),
        ),
        out_specs=(P("tp", None, "req"), P("req", None, "tp")),
        check_vma=False,
    )
```

```python
import math

import jax
import jax.numpy as jnp
from jax import lax
from jax.experimental import pallas as pl
from jax.experimental.pallas import tpu as pltpu
from jax.sharding import PartitionSpec as P

HD = 128


NEG = -1e30


def ancestors(parent):
    tree_size = parent.shape[-1]
    node_ids = lax.broadcasted_iota(jnp.int32, (tree_size, tree_size), 1)
    parent_hot = (parent[..., :, None] == node_ids).astype(jnp.float32)
    reached = jnp.minimum(parent_hot + jnp.eye(tree_size, dtype=jnp.float32), 1.0)
    for rounds in range(max(1, (tree_size - 1).bit_length())):
        reached = jnp.minimum(
            jnp.einsum("rij,rjk->rik", reached, reached, precision=lax.Precision.HIGHEST), 1.0
        )
    return reached


def shards_general(
    queries, tree_kv, tree_parent, accepted_path, cache_kv, piece_owner, cache_len, out_weight
):
    kvheads_local = tree_kv.shape[-1] // (2 * HD)
    heads_local = queries.shape[-1] // HD
    group_size = heads_local // kvheads_local
    tree_size = queries.shape[1]
    slot_count = cache_kv.shape[0]
    piece_rows = cache_kv.shape[1]
    depth_most = accepted_path.shape[1]
    scaling = 1.0 / math.sqrt(HD)
    every_query = lax.all_gather(queries, "req", axis=0, tiled=True)
    req_total = every_query.shape[0]
    owner_req = piece_owner[:, 0]
    owner_piece = piece_owner[:, 1]
    safe_req = jnp.maximum(owner_req, 0)
    slot_query = every_query[safe_req].reshape(slot_count, tree_size, kvheads_local, group_size, HD)
    stored = cache_kv.reshape(slot_count, piece_rows, kvheads_local, 2, HD)
    row_pos = owner_piece[:, None] * piece_rows + lax.broadcasted_iota(
        jnp.int32, (slot_count, piece_rows), 1
    )
    visible = (owner_req >= 0)[:, None] & (row_pos < cache_len[safe_req][:, None])
    wide_mask = visible[:, None, None, None, :]
    scores = (
        jnp.einsum(
            "stkgd,spkd->stkgp", slot_query, stored[:, :, :, 0], preferred_element_type=jnp.float32
        )
        * scaling
    )
    scores = jnp.where(wide_mask, scores, NEG)
    slot_peak = jnp.max(scores, -1)
    expo = jnp.where(wide_mask, jnp.exp(scores - slot_peak[..., None]), 0.0)
    slot_den = jnp.sum(expo, -1)
    weights = expo.astype(jnp.bfloat16)
    slot_num = jnp.einsum(
        "stkgp,spkd->stkgd", weights, stored[:, :, :, 1], preferred_element_type=jnp.float32
    )
    request_ids = lax.broadcasted_iota(jnp.int32, (req_total, slot_count), 0)
    member = (owner_req[None, :] == request_ids)[:, :, None, None, None]
    req_peak = jnp.max(jnp.where(member, slot_peak[None], NEG), axis=1)
    factor = jnp.where(
        member, jnp.exp(jnp.where(member, slot_peak[None] - req_peak[:, None], 0.0)), 0.0
    )
    req_den = jnp.sum(factor * slot_den[None], axis=1)
    req_num = jnp.einsum("rstkg,stkgd->rtkgd", factor, slot_num, precision=lax.Precision.HIGHEST)
    peak_table = req_peak.reshape(req_total, tree_size, heads_local)
    den_table = req_den.reshape(req_total, tree_size, heads_local)
    num_table = req_num.reshape(req_total, tree_size, heads_local * HD)
    own_index = lax.axis_index("req")
    got_peak, got_den, got_num = (
        lax.all_to_all(
            peak_table.astype(jnp.bfloat16), "req", split_axis=0, concat_axis=0, tiled=True
        ).astype(peak_table.dtype),
        lax.all_to_all(
            den_table.astype(jnp.bfloat16), "req", split_axis=0, concat_axis=0, tiled=True
        ).astype(den_table.dtype),
        lax.all_to_all(
            num_table.astype(jnp.bfloat16), "req", split_axis=0, concat_axis=0, tiled=True
        ).astype(num_table.dtype),
    )
    cache_peak = jnp.max(got_peak, axis=0)
    source_scale = jnp.exp(got_peak - cache_peak[None])
    cache_den = jnp.sum(source_scale * got_den, axis=0)
    got_rows = got_num.reshape(got_num.shape[0], tree_size, heads_local, HD)
    cache_num = jnp.sum(source_scale[..., None] * got_rows, axis=0)
    reached = ancestors(tree_parent)[0]
    home_query = queries[0].reshape(tree_size, kvheads_local, group_size, HD)
    fresh = tree_kv[0].reshape(tree_size, kvheads_local, 2, HD)
    tree_mask = reached[:, None, None, :] > 0.5
    tree_scores = (
        jnp.einsum("ikgd,jkd->ikgj", home_query, fresh[:, :, 0], preferred_element_type=jnp.float32)
        * scaling
    )
    tree_scores = jnp.where(tree_mask, tree_scores, NEG)
    tree_peak = jnp.max(tree_scores, -1)
    tree_exp = jnp.where(tree_mask, jnp.exp(tree_scores - tree_peak[..., None]), 0.0)
    tree_den = jnp.sum(tree_exp, -1).reshape(tree_size, heads_local)
    tree_num = jnp.einsum(
        "ikgj,jkd->ikgd",
        tree_exp.astype(jnp.bfloat16),
        fresh[:, :, 1],
        preferred_element_type=jnp.float32,
    )
    tree_num = tree_num.reshape(tree_size, heads_local, HD)
    tree_peak = tree_peak.reshape(tree_size, heads_local)
    total_peak = jnp.maximum(cache_peak, tree_peak)
    cache_scale = jnp.exp(cache_peak - total_peak)
    tree_scale = jnp.exp(tree_peak - total_peak)
    denom = cache_den * cache_scale + tree_den * tree_scale
    numer = cache_num * cache_scale[..., None] + tree_num * tree_scale[..., None]
    attention = (
        (numer / denom[..., None]).reshape(1, tree_size, heads_local * HD).astype(jnp.bfloat16)
    )
    piece = lax.all_gather(attention, "req", axis=0, tiled=True)
    flat_rows = piece.reshape(piece.shape[0] * piece.shape[1], piece.shape[2])
    product = jnp.dot(flat_rows, out_weight, preferred_element_type=jnp.float32)
    terms = product.reshape(piece.shape[0], piece.shape[1], out_weight.shape[1])
    mixed = lax.psum_scatter(terms.astype(jnp.bfloat16), "tp", scatter_dimension=0, tiled=True)
    own_path = lax.dynamic_index_in_dim(accepted_path, own_index, 0, keepdims=False)
    picked = tree_kv[0][jnp.maximum(own_path, 0)]
    picked = jnp.where((own_path >= 0)[:, None], picked, jnp.zeros_like(picked))
    all_rows = lax.all_gather(picked[None], "req", axis=0, tiled=True)
    counts = jnp.sum((accepted_path >= 0).astype(jnp.int32), axis=1)
    offset = row_pos - cache_len[safe_req][:, None]
    writing = (owner_req >= 0)[:, None] & (offset >= 0) & (offset < counts[safe_req][:, None])
    slot_rows = all_rows[safe_req]
    chosen = jnp.take_along_axis(slot_rows, jnp.clip(offset, 0, depth_most - 1)[:, :, None], axis=1)
    cache_out = jnp.where(writing[:, :, None], chosen, cache_kv)
    return (mixed, cache_out)


MESH = pl.DeviceIdType.MESH
PAD = 32
KINDS = 21
VMEM_LIMIT = 63 * 1024 * 1024


def place():
    me = lax.axis_index("req")
    z, y, x = me // 4, (me // 2) % 2, me % 2
    planes = [z, z + 1 - 2 * (z % 2), (z + 2) % 4, 3 - z]
    return me, y, x, planes


def arrivals():
    z = lax.axis_index("req") // 4
    return [z, z + 1 - 2 * (z % 2), 2 - z // 2, 3 - 3 * (z // 2)]


class GridGather:
    def __init__(self, buf, send, recv, part):
        me, y, x, planes = place()
        self.buf, self.send, self.recv, self.part = buf, send, recv, part
        self.column = [plane * 4 + y * 2 + x for plane in arrivals()]
        z = me // 4
        self.inner = (z + 1) // 2 == 1
        self.middle = (3 - z) * 4 + y * 2 + x
        self.to_x, self.to_y = 1 - 2 * x, 2 - 4 * y
        self.near_x, self.near_y = me + self.to_x, me + self.to_y
        self.me = me
        self.sent = []

    def copy(self, origin, piece, target, kind, arrive=None):
        rows = self.buf.shape[1]
        half = rows // 2
        start, size = {"all": (0, rows), "top": (0, half), "low": (half, half)}[piece]
        block = self.buf.at[origin, pl.ds(start, size)]
        return pltpu.make_async_remote_copy(
            src_ref=block,
            dst_ref=block,
            send_sem=self.send.at[self.part, kind],
            recv_sem=self.recv.at[self.part, kind if arrive is None else arrive],
            device_id={"req": target},
            device_id_type=MESH,
        )

    def go(self, *args):
        moving = self.copy(*args)
        moving.start()
        self.sent.append((None, moving))

    def relay(self, *args):
        @pl.when(self.inner)
        def _():
            self.copy(*args).start()

        self.sent.append((self.inner, args))

    def begin(self):
        self.go(self.me, "all", self.column[1], 0, 0)
        self.relay(self.me, "all", self.middle, 1, 1)
        self.step(0)

    def step(self, k):
        column = self.column
        if k < 4:
            if k:
                self.copy(column[k], "all", self.near_x, k - 1).wait_recv()
                if k == 1:
                    self.relay(column[1], "all", self.middle, 2, 2)
                else:
                    self.relay(column[k], "all", column[1], k + 1, k - 1)
            self.go(column[k], "all", self.near_x, 5 + k)
            self.go(column[k], "all", self.near_y, 9 + k)
        if k:
            across_x, across_y = column[k - 1] + self.to_x, column[k - 1] + self.to_y
            self.copy(across_x, "all", self.near_x, 4 + k).wait_recv()
            self.go(across_x, "top", self.near_y, 12 + k)
            self.copy(across_y, "all", self.near_x, 8 + k).wait_recv()
            self.go(across_y, "low", self.near_x, 16 + k)

    def end(self):
        for k in range(4):
            across = self.column[k] + self.to_x + self.to_y
            self.copy(across, "top", self.near_x, 13 + k).wait_recv()
            self.copy(across, "low", self.near_x, 17 + k).wait_recv()

    def finish(self):
        for only, moving in self.sent:
            if only is None:
                moving.wait_send()
                continue

            @pl.when(only)
            def _():
                self.copy(*moving).wait_send()


def iota(shape, dim):
    return lax.broadcasted_iota(jnp.int32, shape, dim)


def as_column(row):
    size = row.shape[1]
    shape = (size, size)
    return jnp.sum(
        jnp.where(iota(shape, 0) == iota(shape, 1), row, 0.0), axis=1, keepdims=True
    )


def attend(query, key, value, mask, scaling, owner):
    rows = query.shape[0]
    scores = scaling * lax.dot_general(
        query, key, (((1,), (1,)), ((), ())), preferred_element_type=jnp.float32
    )
    scores = jnp.where(mask, scores, NEG)
    peak = jnp.max(scores, axis=1, keepdims=True)
    expo = jnp.where(mask, jnp.exp(scores - peak), 0.0)
    denom = jnp.sum(expo, axis=1, keepdims=True)
    numer = jnp.dot(expo.astype(jnp.bfloat16), value, preferred_element_type=jnp.float32)
    some = denom > 0.0
    safe = jnp.where(some, denom, 1.0)
    level = jnp.where(some, peak + jnp.log(safe), NEG)
    out = numer * (1.0 / safe)
    shape = (PAD, HD)
    pick = iota(shape, 0) == iota(shape, 1)
    where = iota(shape, 0)
    blocks = []
    for g in range(rows // PAD):
        line = jnp.sum(
            jnp.where(pick, level[g * PAD : (g + 1) * PAD], 0.0), axis=0, keepdims=True
        )
        high = line.astype(jnp.bfloat16).astype(jnp.float32)
        block = out[g * PAD : (g + 1) * PAD]
        block = jnp.where(where == 28, high, block)
        block = jnp.where(where == 29, line - high, block)
        block = jnp.where(where == 30, owner, block)
        blocks.append(block.astype(jnp.bfloat16))
    return blocks


def layer_kernel(
    owner_h, len_h, parent_h, path_h, query_h, tree_h, cache_h, weight_h,
    mixed_ref, cache_out,
    owner_ref, len_ref, parent_ref, path_ref, path_s, query_ref, tree_ref, cache_v, weight_v,
    gathered_a, gathered_b, packed, tree_f, tree_b, reach_v, outgoing, incoming,
    wide, owners, joined, compact, attn, half_out, half_in,
    local_sem, send1, recv1, send2, recv2, send3, recv3, send4, recv4,
):
    me, y, x, planes = place()
    tp = lax.axis_index("tp")
    gathered = [gathered_a, gathered_b]
    tree_size = query_h.shape[1]
    slots = cache_h.shape[0]
    piece_rows = cache_h.shape[1]
    scaling = 1.0 / math.sqrt(HD)
    pairs = [
        (query_h, query_ref), (tree_h, tree_ref), (path_h, path_ref), (parent_h, parent_ref),
        (owner_h, owner_ref), (len_h, len_ref), (cache_h, cache_v), (weight_h, weight_v),
        (path_h, path_s),
    ]
    loads = [
        pltpu.make_async_copy(there, here, local_sem.at[n])
        for n, (there, here) in enumerate(pairs)
    ]
    for load in loads:
        load.start()

    barrier = pltpu.get_barrier_semaphore()
    for d in range(1, 16):
        pl.semaphore_signal(
            barrier, inc=1, device_id={"req": (me + d) % 16}, device_id_type=MESH
        )
    pl.semaphore_signal(barrier, inc=1, device_id={"tp": 1 - tp}, device_id_type=MESH)

    for load in loads[:3]:
        load.wait()
    tree_f[...] = jnp.zeros_like(tree_f)
    tree_f[0:tree_size] = tree_ref[0].astype(jnp.float32)
    tree_b[...] = tree_f[...].astype(jnp.bfloat16)
    table = path_ref[...].astype(jnp.float32)
    path = jnp.sum(jnp.where(iota(table.shape, 1) == me, table, 0.0), axis=1, keepdims=True)
    depth = path.shape[0]
    chosen = (path == iota((depth, PAD), 1).astype(jnp.float32)).astype(jnp.bfloat16)
    picked = jnp.dot(chosen, tree_b[...], preferred_element_type=jnp.float32)
    width = tree_h.shape[2]
    packed[0:tree_size] = query_ref[0].astype(jnp.float32)
    packed[tree_size:PAD, 0:width] = picked[0:4]
    packed[tree_size:PAD, width : 2 * width] = picked[4:8]
    for c in range(2):
        gathered[c][me] = packed[:, c * width : (c + 1) * width].astype(jnp.bfloat16)

    pl.semaphore_wait(barrier, 16)
    first = [GridGather(gathered[c], send1, recv1, c) for c in range(2)]
    first[0].begin()
    first[0].step(1)
    first[1].begin()
    first[0].step(2)
    first[0].step(3)
    first[1].step(1)

    loads[3].wait()
    parent = as_column(parent_ref[...].astype(jnp.float32))
    lanes = iota((tree_size, PAD), 1).astype(jnp.float32)
    reach_v[...] = (iota((PAD, PAD), 0) == iota((PAD, PAD), 1)).astype(jnp.float32)
    reach_v[0:tree_size] = jnp.minimum(
        reach_v[0:tree_size] + (parent == lanes).astype(jnp.float32), 1.0
    )
    reached = reach_v[...]
    for rounds in range(max(1, (tree_size - 1).bit_length())):
        short = reached.astype(jnp.bfloat16)
        reached = jnp.minimum(jnp.dot(short, short, preferred_element_type=jnp.float32), 1.0)
    tree_mask = jnp.concatenate([reached] * 4, axis=0) > 0.5
    first[0].step(4)
    first[1].step(2)
    for load in loads[4:7]:
        load.wait()

    sent = []

    def attend_head(kv):
        c, offset = kv // 2, (kv % 2) * 4 * HD
        for s in range(slots + 1):
            if s < slots:
                owner = owner_ref[0, s]
                request = jnp.maximum(owner, 0)
                limit = jnp.where(owner >= 0, len_ref[request] - owner_ref[1, s] * piece_rows, 0)
                mask = iota((4 * PAD, piece_rows), 1) < limit
                source, keys = request, cache_v.at[s]
            else:
                owner, source, keys, mask = me, me, tree_b, tree_mask
            wide_q = gathered[c][source, :, offset : offset + 4 * HD]
            query = jnp.concatenate([wide_q[:, g * HD : (g + 1) * HD] for g in range(4)], axis=0)
            at = kv * 2 * HD
            blocks = attend(
                query, keys[:, at : at + HD], keys[:, at + HD : at + 2 * HD], mask, scaling,
                owner.astype(jnp.float32),
            )
            for g in range(4):
                outgoing[kv, g, s * PAD : (s + 1) * PAD] = blocks[g]
        for k in range(4):
            plane = planes[k]
            target = plane * 4 + kv

            def remote(target=target, plane=plane, k=k):
                return pltpu.make_async_remote_copy(
                    src_ref=outgoing.at[kv, plane],
                    dst_ref=incoming.at[me],
                    send_sem=send2.at[kv, k],
                    recv_sem=recv2.at[me],
                    device_id={"req": target},
                    device_id_type=MESH,
                )

            if k == 0:

                @pl.when(target != me)
                def _():
                    remote().start()

                @pl.when(target == me)
                def _():
                    incoming[me] = outgoing[kv, plane]

            else:
                remote().start()
            sent.append((k, target, remote))

    first[0].end()
    attend_head(0)
    first[1].step(3)
    attend_head(1)
    first[1].step(4)
    first[1].end()
    attend_head(2)
    attend_head(3)
    loads[8].wait()
    saves = [
        pltpu.make_async_copy(cache_v.at[s], cache_out.at[s], local_sem.at[9 + s])
        for s in range(slots)
    ]
    span = 64
    for s in range(slots):
        owner = owner_ref[0, s]
        request = jnp.maximum(owner, 0)
        begin = len_ref[request] - owner_ref[1, s] * piece_rows
        count = jnp.int32(0)
        for j in range(depth):
            count = count + (path_s[j, request] >= 0).astype(jnp.int32)
        count = jnp.where(owner >= 0, count, 0)
        spare = [gathered[c][request, 16:32, :] for c in range(2)]
        for row in range(0, piece_rows, span):
            offset = iota((span, 16), 0) + (row - begin)
            lane = iota((span, 16), 1) - 12
            low = ((offset == lane) & (lane >= 0)).astype(jnp.bfloat16)
            high = ((offset == lane + 4) & (lane >= 0)).astype(jnp.bfloat16)
            accepted = jnp.dot(
                low, spare[0], preferred_element_type=jnp.float32
            ) + jnp.dot(high, spare[1], preferred_element_type=jnp.float32)
            offset = iota((span, width), 0) + (row - begin)
            writing = (offset >= 0) & (offset < count)
            old = cache_v[s, row : row + span, :].astype(jnp.float32)
            cache_v[s, row : row + span, :] = jnp.where(writing, accepted, old).astype(jnp.bfloat16)
        saves[s].start()
    for d in range(1, 16):
        source = (me + d) % 16
        pltpu.make_async_remote_copy(
            src_ref=outgoing.at[0, 0],
            dst_ref=incoming.at[source],
            send_sem=send2.at[0, 0],
            recv_sem=recv2.at[source],
            device_id={"req": source},
            device_id_type=MESH,
        ).wait_recv()

    pieces = 16 * (slots + 1)
    wide[...] = incoming[...].astype(jnp.float32).reshape(pieces * PAD, HD)
    level = wide[pl.ds(28, pieces, stride=PAD), :] + wide[pl.ds(29, pieces, stride=PAD), :]
    holder = wide[pl.ds(30, pieces, stride=PAD), :]
    owners[...] = holder
    share = jnp.zeros_like(level)
    for r in range(16):
        member = holder == float(r)
        peak = jnp.max(jnp.where(member, level, NEG), axis=0, keepdims=True)
        expo = jnp.where(member, jnp.exp(jnp.where(member, level - peak, 0.0)), 0.0)
        share = share + expo * (1.0 / jnp.sum(expo, axis=0, keepdims=True))
    turned = share.T
    for b in range(pieces):
        block = slice(b * PAD, (b + 1) * PAD)
        wide[block] = wide[block] * turned[0:PAD, b : b + 1]

    def join_half(part, to):
        def join(i, carry):
            r = part * 8 + i
            mine = r.astype(jnp.float32)
            first_row = pl.multiple_of((r * (slots + 1) + slots) * PAD, PAD)
            total = wide[pl.ds(first_row, PAD), :]
            for b in range(pieces):
                if b % (slots + 1) < slots:
                    total = total + jnp.where(
                        owners[b : b + 1] == mine, wide[b * PAD : (b + 1) * PAD], 0.0
                    )
            joined[i] = total
            return carry

        lax.fori_loop(0, 8, join, 0)
        for i in range(8):
            compact[pl.ds(i, tree_size, stride=8), :] = joined[i, 0:tree_size]
        attn[to, me] = compact[...].astype(jnp.bfloat16)

    last = [GridGather(attn.at[c], send3, recv3, c) for c in range(2)]
    join_half(1 - tp, 0)
    last[0].begin()
    join_half(tp, 1)
    last[0].step(1)
    last[1].begin()
    last[0].step(2)
    last[1].step(1)
    last[0].step(3)
    last[1].step(2)
    last[0].step(4)
    last[1].step(3)
    loads[7].wait()

    def project(part):
        total = jnp.zeros(half_out.shape, jnp.float32)
        for kv in range(4):
            for g in range(0, 4, 2):
                head = 4 * kv + g
                pair = jnp.concatenate(
                    [attn[part, 4 * g + kv], attn[part, 4 * g + 4 + kv]], axis=1
                )
                total = total + jnp.dot(
                    pair, weight_v[head * HD : (head + 2) * HD],
                    preferred_element_type=jnp.float32,
                )
        return total

    last[0].end()
    last[1].step(4)
    half_out[...] = project(0).astype(jnp.bfloat16)
    swap = pltpu.make_async_remote_copy(
        src_ref=half_out,
        dst_ref=half_in,
        send_sem=send4,
        recv_sem=recv4,
        device_id={"tp": 1 - tp},
        device_id_type=MESH,
    )
    swap.start()
    last[1].end()
    own_half = project(1)
    swap.wait_recv()
    mixed_ref[...] = (own_half + half_in[...].astype(jnp.float32)).astype(jnp.bfloat16)

    swap.wait_send()
    for save in saves:
        save.wait()
    for gather in first + last:
        gather.finish()
    for k, target, remote in sent:
        if k == 0:

            @pl.when(target != me)
            def _():
                remote().wait_send()

        else:
            remote().wait_send()


def shards_grid(
    queries, tree_kv, tree_parent, accepted_path, cache_kv, piece_owner, cache_len, out_weight
):
    slots, piece_rows, width = cache_kv.shape
    tree_size = queries.shape[1]
    columns = queries.shape[2]
    reqs = 16
    half = reqs * tree_size // 2
    vmem = pl.BlockSpec(memory_space=pltpu.VMEM)
    hbm = pl.BlockSpec(memory_space=pltpu.HBM)
    pieces = reqs * (slots + 1)
    dma = pltpu.SemaphoreType.DMA
    bf16, f32, i32 = jnp.bfloat16, jnp.float32, jnp.int32
    owner_t, path_t = piece_owner.T, accepted_path.T
    mixed, cache_out = pl.pallas_call(
        layer_kernel,
        out_shape=(
            jax.ShapeDtypeStruct((half, out_weight.shape[1]), bf16),
            jax.ShapeDtypeStruct(cache_kv.shape, bf16),
        ),
        in_specs=[hbm] * 8,
        out_specs=(vmem, hbm),
        scratch_shapes=[
            pltpu.SMEM(owner_t.shape, i32),
            pltpu.SMEM(cache_len.shape, i32),
            pltpu.VMEM(tree_parent.shape, i32),
            pltpu.VMEM(path_t.shape, i32),
            pltpu.SMEM(path_t.shape, i32),
            pltpu.VMEM(queries.shape, bf16),
            pltpu.VMEM(tree_kv.shape, bf16),
            pltpu.VMEM(cache_kv.shape, bf16),
            pltpu.VMEM(out_weight.shape, bf16),
            pltpu.VMEM((reqs, PAD, columns // 2), bf16),
            pltpu.VMEM((reqs, PAD, columns // 2), bf16),
            pltpu.VMEM((PAD, columns), f32),
            pltpu.VMEM((PAD, width), f32),
            pltpu.VMEM((PAD, width), bf16),
            pltpu.VMEM((PAD, PAD), f32),
            pltpu.VMEM((4, 4, (slots + 1) * PAD, HD), bf16),
            pltpu.VMEM((reqs, (slots + 1) * PAD, HD), bf16),
            pltpu.VMEM((pieces * PAD, HD), f32),
            pltpu.VMEM((pieces, HD), f32),
            pltpu.VMEM((reqs // 2, PAD, HD), f32),
            pltpu.VMEM((half, HD), f32),
            pltpu.VMEM((2, reqs, half, HD), bf16),
            pltpu.VMEM((half, out_weight.shape[1]), bf16),
            pltpu.VMEM((half, out_weight.shape[1]), bf16),
            dma((9 + slots,)),
            dma((2, KINDS)),
            dma((2, KINDS)),
            dma((4, 4)),
            dma((reqs,)),
            dma((2, KINDS)),
            dma((2, KINDS)),
            dma,
            dma,
        ],
        compiler_params=pltpu.CompilerParams(
            collective_id=0, has_side_effects=True, vmem_limit_bytes=VMEM_LIMIT
        ),
    )(owner_t, cache_len, tree_parent, path_t, queries, tree_kv, cache_kv, out_weight)
    mixed = mixed.reshape(tree_size, reqs // 2, out_weight.shape[1]).transpose(1, 0, 2)
    return mixed, cache_out


def solution(mesh):
    body = shards_grid if dict(mesh.shape) == {"req": 16, "tp": 2} else shards_general
    return jax.shard_map(
        body,
        mesh=mesh,
        in_specs=(
            P("req", None, "tp"),
            P("req", None, "tp"),
            P("req", None),
            P(),
            P("req", None, "tp"),
            P("req", None),
            P(),
            P("tp", "req"),
        ),
        out_specs=(P("tp", None, "req"), P("req", None, "tp")),
        check_vma=False,
    )
```

```python
import math

import jax
import jax.numpy as jnp
from jax import lax
from jax.experimental import pallas as pl
from jax.experimental.pallas import tpu as pltpu
from jax.sharding import PartitionSpec as P

HD = 128


NEG = -1e30


def ancestors(parent):
    tree_size = parent.shape[-1]
    node_ids = lax.broadcasted_iota(jnp.int32, (tree_size, tree_size), 1)
    parent_hot = (parent[..., :, None] == node_ids).astype(jnp.float32)
    reached = jnp.minimum(parent_hot + jnp.eye(tree_size, dtype=jnp.float32), 1.0)
    for rounds in range(max(1, (tree_size - 1).bit_length())):
        reached = jnp.minimum(
            jnp.einsum("rij,rjk->rik", reached, reached, precision=lax.Precision.HIGHEST), 1.0
        )
    return reached


def shards_general(
    queries, tree_kv, tree_parent, accepted_path, cache_kv, piece_owner, cache_len, out_weight
):
    kvheads_local = tree_kv.shape[-1] // (2 * HD)
    heads_local = queries.shape[-1] // HD
    group_size = heads_local // kvheads_local
    tree_size = queries.shape[1]
    slot_count = cache_kv.shape[0]
    piece_rows = cache_kv.shape[1]
    depth_most = accepted_path.shape[1]
    scaling = 1.0 / math.sqrt(HD)
    every_query = lax.all_gather(queries, "req", axis=0, tiled=True)
    req_total = every_query.shape[0]
    owner_req = piece_owner[:, 0]
    owner_piece = piece_owner[:, 1]
    safe_req = jnp.maximum(owner_req, 0)
    slot_query = every_query[safe_req].reshape(slot_count, tree_size, kvheads_local, group_size, HD)
    stored = cache_kv.reshape(slot_count, piece_rows, kvheads_local, 2, HD)
    row_pos = owner_piece[:, None] * piece_rows + lax.broadcasted_iota(
        jnp.int32, (slot_count, piece_rows), 1
    )
    visible = (owner_req >= 0)[:, None] & (row_pos < cache_len[safe_req][:, None])
    wide_mask = visible[:, None, None, None, :]
    scores = (
        jnp.einsum(
            "stkgd,spkd->stkgp", slot_query, stored[:, :, :, 0], preferred_element_type=jnp.float32
        )
        * scaling
    )
    scores = jnp.where(wide_mask, scores, NEG)
    slot_peak = jnp.max(scores, -1)
    expo = jnp.where(wide_mask, jnp.exp(scores - slot_peak[..., None]), 0.0)
    slot_den = jnp.sum(expo, -1)
    weights = expo.astype(jnp.bfloat16)
    slot_num = jnp.einsum(
        "stkgp,spkd->stkgd", weights, stored[:, :, :, 1], preferred_element_type=jnp.float32
    )
    request_ids = lax.broadcasted_iota(jnp.int32, (req_total, slot_count), 0)
    member = (owner_req[None, :] == request_ids)[:, :, None, None, None]
    req_peak = jnp.max(jnp.where(member, slot_peak[None], NEG), axis=1)
    factor = jnp.where(
        member, jnp.exp(jnp.where(member, slot_peak[None] - req_peak[:, None], 0.0)), 0.0
    )
    req_den = jnp.sum(factor * slot_den[None], axis=1)
    req_num = jnp.einsum("rstkg,stkgd->rtkgd", factor, slot_num, precision=lax.Precision.HIGHEST)
    peak_table = req_peak.reshape(req_total, tree_size, heads_local)
    den_table = req_den.reshape(req_total, tree_size, heads_local)
    num_table = req_num.reshape(req_total, tree_size, heads_local * HD)
    own_index = lax.axis_index("req")
    got_peak, got_den, got_num = (
        lax.all_to_all(
            peak_table.astype(jnp.bfloat16), "req", split_axis=0, concat_axis=0, tiled=True
        ).astype(peak_table.dtype),
        lax.all_to_all(
            den_table.astype(jnp.bfloat16), "req", split_axis=0, concat_axis=0, tiled=True
        ).astype(den_table.dtype),
        lax.all_to_all(
            num_table.astype(jnp.bfloat16), "req", split_axis=0, concat_axis=0, tiled=True
        ).astype(num_table.dtype),
    )
    cache_peak = jnp.max(got_peak, axis=0)
    source_scale = jnp.exp(got_peak - cache_peak[None])
    cache_den = jnp.sum(source_scale * got_den, axis=0)
    got_rows = got_num.reshape(got_num.shape[0], tree_size, heads_local, HD)
    cache_num = jnp.sum(source_scale[..., None] * got_rows, axis=0)
    reached = ancestors(tree_parent)[0]
    home_query = queries[0].reshape(tree_size, kvheads_local, group_size, HD)
    fresh = tree_kv[0].reshape(tree_size, kvheads_local, 2, HD)
    tree_mask = reached[:, None, None, :] > 0.5
    tree_scores = (
        jnp.einsum("ikgd,jkd->ikgj", home_query, fresh[:, :, 0], preferred_element_type=jnp.float32)
        * scaling
    )
    tree_scores = jnp.where(tree_mask, tree_scores, NEG)
    tree_peak = jnp.max(tree_scores, -1)
    tree_exp = jnp.where(tree_mask, jnp.exp(tree_scores - tree_peak[..., None]), 0.0)
    tree_den = jnp.sum(tree_exp, -1).reshape(tree_size, heads_local)
    tree_num = jnp.einsum(
        "ikgj,jkd->ikgd",
        tree_exp.astype(jnp.bfloat16),
        fresh[:, :, 1],
        preferred_element_type=jnp.float32,
    )
    tree_num = tree_num.reshape(tree_size, heads_local, HD)
    tree_peak = tree_peak.reshape(tree_size, heads_local)
    total_peak = jnp.maximum(cache_peak, tree_peak)
    cache_scale = jnp.exp(cache_peak - total_peak)
    tree_scale = jnp.exp(tree_peak - total_peak)
    denom = cache_den * cache_scale + tree_den * tree_scale
    numer = cache_num * cache_scale[..., None] + tree_num * tree_scale[..., None]
    attention = (
        (numer / denom[..., None]).reshape(1, tree_size, heads_local * HD).astype(jnp.bfloat16)
    )
    piece = lax.all_gather(attention, "req", axis=0, tiled=True)
    flat_rows = piece.reshape(piece.shape[0] * piece.shape[1], piece.shape[2])
    product = jnp.dot(flat_rows, out_weight, preferred_element_type=jnp.float32)
    terms = product.reshape(piece.shape[0], piece.shape[1], out_weight.shape[1])
    mixed = lax.psum_scatter(terms.astype(jnp.bfloat16), "tp", scatter_dimension=0, tiled=True)
    own_path = lax.dynamic_index_in_dim(accepted_path, own_index, 0, keepdims=False)
    picked = tree_kv[0][jnp.maximum(own_path, 0)]
    picked = jnp.where((own_path >= 0)[:, None], picked, jnp.zeros_like(picked))
    all_rows = lax.all_gather(picked[None], "req", axis=0, tiled=True)
    counts = jnp.sum((accepted_path >= 0).astype(jnp.int32), axis=1)
    offset = row_pos - cache_len[safe_req][:, None]
    writing = (owner_req >= 0)[:, None] & (offset >= 0) & (offset < counts[safe_req][:, None])
    slot_rows = all_rows[safe_req]
    chosen = jnp.take_along_axis(slot_rows, jnp.clip(offset, 0, depth_most - 1)[:, :, None], axis=1)
    cache_out = jnp.where(writing[:, :, None], chosen, cache_kv)
    return (mixed, cache_out)


MESH = pl.DeviceIdType.MESH
PAD = 32
KINDS = 21
VMEM_LIMIT = 63 * 1024 * 1024


def place():
    me = lax.axis_index("req")
    z, y, x = me // 4, (me // 2) % 2, me % 2
    planes = [z, z + 1 - 2 * (z % 2), (z + 2) % 4, 3 - z]
    return me, y, x, planes


def arrivals():
    z = lax.axis_index("req") // 4
    return [z, z + 1 - 2 * (z % 2), 2 - z // 2, 3 - 3 * (z // 2)]


class GridGather:
    def __init__(self, buf, send, recv, part):
        me, y, x, planes = place()
        self.buf, self.send, self.recv, self.part = buf, send, recv, part
        self.column = [plane * 4 + y * 2 + x for plane in arrivals()]
        z = me // 4
        self.inner = (z + 1) // 2 == 1
        self.middle = (3 - z) * 4 + y * 2 + x
        self.to_x, self.to_y = 1 - 2 * x, 2 - 4 * y
        self.near_x, self.near_y = me + self.to_x, me + self.to_y
        self.me = me
        self.sent = []

    def copy(self, origin, piece, target, kind, arrive=None):
        rows = self.buf.shape[1]
        half = rows // 2
        start, size = {"all": (0, rows), "top": (0, half), "low": (half, half)}[piece]
        block = self.buf.at[origin, pl.ds(start, size)]
        return pltpu.make_async_remote_copy(
            src_ref=block,
            dst_ref=block,
            send_sem=self.send.at[self.part, kind],
            recv_sem=self.recv.at[self.part, kind if arrive is None else arrive],
            device_id={"req": target},
            device_id_type=MESH,
        )

    def go(self, *args):
        moving = self.copy(*args)
        moving.start()
        self.sent.append((None, moving))

    def relay(self, *args):
        @pl.when(self.inner)
        def _():
            self.copy(*args).start()

        self.sent.append((self.inner, args))

    def begin(self):
        self.go(self.me, "all", self.column[1], 0, 0)
        self.relay(self.me, "all", self.middle, 1, 1)
        self.step(0)

    def step(self, k):
        column = self.column
        if k < 4:
            if k:
                self.copy(column[k], "all", self.near_x, k - 1).wait_recv()
                if k == 1:
                    self.relay(column[1], "all", self.middle, 2, 2)
                else:
                    self.relay(column[k], "all", column[1], k + 1, k - 1)
            self.go(column[k], "all", self.near_x, 5 + k)
            self.go(column[k], "all", self.near_y, 9 + k)
        if k:
            across_x, across_y = column[k - 1] + self.to_x, column[k - 1] + self.to_y
            self.copy(across_x, "all", self.near_x, 4 + k).wait_recv()
            self.go(across_x, "top", self.near_y, 12 + k)
            self.copy(across_y, "all", self.near_x, 8 + k).wait_recv()
            self.go(across_y, "low", self.near_x, 16 + k)

    def end(self):
        for k in range(4):
            across = self.column[k] + self.to_x + self.to_y
            self.copy(across, "top", self.near_x, 13 + k).wait_recv()
            self.copy(across, "low", self.near_x, 17 + k).wait_recv()

    def finish(self):
        for only, moving in self.sent:
            if only is None:
                moving.wait_send()
                continue

            @pl.when(only)
            def _():
                self.copy(*moving).wait_send()


def iota(shape, dim):
    return lax.broadcasted_iota(jnp.int32, shape, dim)


def as_column(row):
    size = row.shape[1]
    shape = (size, size)
    return jnp.sum(
        jnp.where(iota(shape, 0) == iota(shape, 1), row, 0.0), axis=1, keepdims=True
    )


def attend(query, key, value, mask, scaling, owner):
    rows = query.shape[0]
    scores = scaling * lax.dot_general(
        query, key, (((1,), (1,)), ((), ())), preferred_element_type=jnp.float32
    )
    scores = jnp.where(mask, scores, NEG)
    peak = jnp.max(scores, axis=1, keepdims=True)
    expo = jnp.where(mask, jnp.exp(scores - peak), 0.0)
    denom = jnp.sum(expo, axis=1, keepdims=True)
    numer = jnp.dot(expo.astype(jnp.bfloat16), value, preferred_element_type=jnp.float32)
    some = denom > 0.0
    safe = jnp.where(some, denom, 1.0)
    level = jnp.where(some, peak + jnp.log(safe), NEG)
    out = numer * (1.0 / safe)
    shape = (PAD, HD)
    pick = iota(shape, 0) == iota(shape, 1)
    where = iota(shape, 0)
    blocks = []
    for g in range(rows // PAD):
        line = jnp.sum(
            jnp.where(pick, level[g * PAD : (g + 1) * PAD], 0.0), axis=0, keepdims=True
        )
        high = line.astype(jnp.bfloat16).astype(jnp.float32)
        block = out[g * PAD : (g + 1) * PAD]
        block = jnp.where(where == 28, high, block)
        block = jnp.where(where == 29, line - high, block)
        block = jnp.where(where == 30, owner, block)
        blocks.append(block.astype(jnp.bfloat16))
    return blocks


def layer_kernel(
    owner_h, len_h, parent_h, path_h, query_h, tree_h, cache_h, weight_h,
    mixed_ref, rows_ref,
    owner_ref, owner_v, len_ref, parent_ref, path_ref, query_ref, tree_ref, cache_v, weight_v,
    own_heads, owned, known_v, known, staged, asked, packed, tree_f, tree_b, reach_v, outgoing, incoming,
    wide, owners, joined, compact, attn, half_out, half_in,
    local_sem, send0, recv0, send5, recv5, send1, recv1, send2, recv2, send3, recv3, send4, recv4,
):
    me, y, x, planes = place()
    tp = lax.axis_index("tp")
    tree_size = query_h.shape[1]
    slots = cache_h.shape[0]
    piece_rows = cache_h.shape[1]
    scaling = 1.0 / math.sqrt(HD)
    pairs = [
        (query_h, query_ref), (tree_h, tree_ref), (path_h, path_ref), (parent_h, parent_ref),
        (owner_h, owner_ref), (len_h, len_ref), (cache_h, cache_v), (weight_h, weight_v),
        (owner_h, owner_v),
    ]
    loads = [
        pltpu.make_async_copy(there, here, local_sem.at[n])
        for n, (there, here) in enumerate(pairs)
    ]
    for load in loads:
        load.start()

    barrier = pltpu.get_barrier_semaphore()
    for d in range(1, 16):
        pl.semaphore_signal(
            barrier, inc=1, device_id={"req": (me + d) % 16}, device_id_type=MESH
        )
    pl.semaphore_signal(barrier, inc=1, device_id={"tp": 1 - tp}, device_id_type=MESH)

    for load in loads[:3] + loads[8:9]:
        load.wait()
    tree_f[...] = jnp.zeros_like(tree_f)
    tree_f[0:tree_size] = tree_ref[0].astype(jnp.float32)
    tree_b[...] = tree_f[...].astype(jnp.bfloat16)
    table = path_ref[...].astype(jnp.float32)
    path = jnp.sum(jnp.where(iota(table.shape, 1) == me, table, 0.0), axis=1, keepdims=True)
    depth = path.shape[0]
    chosen = (path == iota((depth, PAD), 1).astype(jnp.float32)).astype(jnp.bfloat16)
    picked = jnp.dot(chosen, tree_b[...], preferred_element_type=jnp.float32)
    width = tree_h.shape[2]
    packed[0:tree_size] = query_ref[0].astype(jnp.float32)
    packed[tree_size:PAD, 0:width] = picked[0:4]
    packed[tree_size:PAD, width : 2 * width] = picked[4:8]
    for head in range(16):
        device = 4 * (head % 4) + head // 4
        own_heads[device] = packed[:, head * HD : (head + 1) * HD].astype(jnp.bfloat16)
    owned[me] = own_heads[me]
    known_v[me] = jnp.zeros(known_v.shape[1:], jnp.int32)
    known_v[me, 0:1, 0:slots] = owner_v[0:1, :]

    pl.semaphore_wait(barrier, 16)

    others = []
    for k in range(4):
        for c in range(4):
            others.append((planes[k] * 4 + (me + c) % 4, k + c > 0))
    others = [device for device, other in others if other]
    hops = []

    def post(block, to, target, send, recv, n):
        moving = pltpu.make_async_remote_copy(
            src_ref=block,
            dst_ref=to,
            send_sem=send.at[n],
            recv_sem=recv.at[me],
            device_id={"req": target},
            device_id_type=MESH,
        )
        moving.start()
        hops.append(moving)

    def take(block, send, recv, source):
        pltpu.make_async_remote_copy(
            src_ref=block,
            dst_ref=block,
            send_sem=send.at[0],
            recv_sem=recv.at[source],
            device_id={"req": (me + 1) % 16},
            device_id_type=MESH,
        ).wait_recv()

    for n, target in enumerate(others):
        post(known_v.at[me], known_v.at[me], target, send0, recv0, n)
    for n, target in enumerate(others):
        post(own_heads.at[target], owned.at[me], target, send1, recv1, n)

    loads[3].wait()
    parent = as_column(parent_ref[...].astype(jnp.float32))
    lanes = iota((tree_size, PAD), 1).astype(jnp.float32)
    reach_v[...] = (iota((PAD, PAD), 0) == iota((PAD, PAD), 1)).astype(jnp.float32)
    reach_v[0:tree_size] = jnp.minimum(
        reach_v[0:tree_size] + (parent == lanes).astype(jnp.float32), 1.0
    )
    reached = reach_v[...]
    for rounds in range(max(1, (tree_size - 1).bit_length())):
        short = reached.astype(jnp.bfloat16)
        reached = jnp.minimum(jnp.dot(short, short, preferred_element_type=jnp.float32), 1.0)
    tree_mask = jnp.concatenate([reached] * 4, axis=0) > 0.5
    for load in loads[4:7]:
        load.wait()
    for source in others:
        take(known_v.at[source], send0, recv0, source)
    table = pltpu.make_async_copy(known_v, known, local_sem.at[9])
    table.start()
    table.wait()
    for source in others:
        take(owned.at[source], send1, recv1, source)

    def stage(device, to):
        for s in range(slots):
            request = jnp.maximum(known[device, 0, s], 0)
            to[s * PAD : (s + 1) * PAD] = owned[request]

    for n, target in enumerate(others):
        stage(target, staged.at[n])
        post(staged.at[n], asked.at[me], target, send5, recv5, n)
    stage(me, asked.at[me])

    sent = []

    def attend_head(kv):
        for g in range(4):
            source = 4 * g + kv

            @pl.when(source != me)
            def _():
                take(asked.at[source], send5, recv5, source)

        for s in range(slots + 1):
            if s < slots:
                owner = owner_ref[0, s]
                request = jnp.maximum(owner, 0)
                limit = jnp.where(owner >= 0, len_ref[request] - owner_ref[1, s] * piece_rows, 0)
                mask = iota((4 * PAD, piece_rows), 1) < limit
                keys = cache_v.at[s]
                parts = [asked[4 * g + kv, s * PAD : (s + 1) * PAD, :] for g in range(4)]
            else:
                owner, keys, mask = me, tree_b, tree_mask
                parts = [own_heads[4 * g + kv] for g in range(4)]
            query = jnp.concatenate(parts, axis=0)
            at = kv * 2 * HD
            blocks = attend(
                query, keys[:, at : at + HD], keys[:, at + HD : at + 2 * HD], mask, scaling,
                owner.astype(jnp.float32),
            )
            for g in range(4):
                outgoing[kv, g, s * PAD : (s + 1) * PAD] = blocks[g]
        for k in range(4):
            plane = planes[k]
            target = plane * 4 + kv

            def remote(target=target, plane=plane, k=k):
                return pltpu.make_async_remote_copy(
                    src_ref=outgoing.at[kv, plane],
                    dst_ref=incoming.at[me],
                    send_sem=send2.at[kv, k],
                    recv_sem=recv2.at[me],
                    device_id={"req": target},
                    device_id_type=MESH,
                )

            if k == 0:

                @pl.when(target != me)
                def _():
                    remote().start()

                @pl.when(target == me)
                def _():
                    incoming[me] = outgoing[kv, plane]

            else:
                remote().start()
            sent.append((k, target, remote))

    for kv in range(4):
        attend_head(kv)
    for s in range(slots):
        for head in range(16):
            device = 4 * (head % 4) + head // 4
            rows_ref[s, :, head * HD : (head + 1) * HD] = asked[
                device, s * PAD + 16 : (s + 1) * PAD, :
            ]
    for d in range(1, 16):
        source = (me + d) % 16
        pltpu.make_async_remote_copy(
            src_ref=outgoing.at[0, 0],
            dst_ref=incoming.at[source],
            send_sem=send2.at[0, 0],
            recv_sem=recv2.at[source],
            device_id={"req": source},
            device_id_type=MESH,
        ).wait_recv()

    pieces = 16 * (slots + 1)
    wide[...] = incoming[...].astype(jnp.float32).reshape(pieces * PAD, HD)
    level = wide[pl.ds(28, pieces, stride=PAD), :] + wide[pl.ds(29, pieces, stride=PAD), :]
    holder = wide[pl.ds(30, pieces, stride=PAD), :]
    owners[...] = holder
    share = jnp.zeros_like(level)
    for r in range(16):
        member = holder == float(r)
        peak = jnp.max(jnp.where(member, level, NEG), axis=0, keepdims=True)
        expo = jnp.where(member, jnp.exp(jnp.where(member, level - peak, 0.0)), 0.0)
        share = share + expo * (1.0 / jnp.sum(expo, axis=0, keepdims=True))
    turned = share.T
    for b in range(pieces):
        block = slice(b * PAD, (b + 1) * PAD)
        wide[block] = wide[block] * turned[0:PAD, b : b + 1]

    def join_half(part, to):
        def join(i, carry):
            r = part * 8 + i
            mine = r.astype(jnp.float32)
            first_row = pl.multiple_of((r * (slots + 1) + slots) * PAD, PAD)
            total = wide[pl.ds(first_row, PAD), :]
            for b in range(pieces):
                if b % (slots + 1) < slots:
                    total = total + jnp.where(
                        owners[b : b + 1] == mine, wide[b * PAD : (b + 1) * PAD], 0.0
                    )
            joined[i] = total
            return carry

        lax.fori_loop(0, 8, join, 0)
        for i in range(8):
            compact[pl.ds(i, tree_size, stride=8), :] = joined[i, 0:tree_size]
        attn[to, me] = compact[...].astype(jnp.bfloat16)

    last = [GridGather(attn.at[c], send3, recv3, c) for c in range(2)]
    join_half(1 - tp, 0)
    last[0].begin()
    join_half(tp, 1)
    last[0].step(1)
    last[1].begin()
    last[0].step(2)
    last[1].step(1)
    last[0].step(3)
    last[1].step(2)
    last[0].step(4)
    last[1].step(3)
    loads[7].wait()

    def project(part):
        total = jnp.zeros(half_out.shape, jnp.float32)
        for kv in range(4):
            for g in range(0, 4, 2):
                head = 4 * kv + g
                pair = jnp.concatenate(
                    [attn[part, 4 * g + kv], attn[part, 4 * g + 4 + kv]], axis=1
                )
                total = total + jnp.dot(
                    pair, weight_v[head * HD : (head + 2) * HD],
                    preferred_element_type=jnp.float32,
                )
        return total

    last[0].end()
    last[1].step(4)
    half_out[...] = project(0).astype(jnp.bfloat16)
    swap = pltpu.make_async_remote_copy(
        src_ref=half_out,
        dst_ref=half_in,
        send_sem=send4,
        recv_sem=recv4,
        device_id={"tp": 1 - tp},
        device_id_type=MESH,
    )
    swap.start()
    last[1].end()
    own_half = project(1)
    swap.wait_recv()
    mixed_ref[...] = (own_half + half_in[...].astype(jnp.float32)).astype(jnp.bfloat16)

    swap.wait_send()
    for hop in hops:
        hop.wait_send()
    for gather in last:
        gather.finish()
    for k, target, remote in sent:
        if k == 0:

            @pl.when(target != me)
            def _():
                remote().wait_send()

        else:
            remote().wait_send()


def append_kernel(
    owner_h, len_h, path_h, cache_ref, rows_h, out_ref,
    owner_ref, len_ref, path_ref, rows_ref, sems, *held,
):
    slots, piece_rows, width = cache_ref.shape
    span = 32
    loads = [pltpu.make_async_copy(cache_ref.at[s], held[s], sems.at[s]) for s in range(slots)]
    stores = [
        pltpu.make_async_copy(held[s], out_ref.at[s], sems.at[slots + s]) for s in range(slots)
    ]
    pairs = [(owner_h, owner_ref), (len_h, len_ref), (path_h, path_ref), (rows_h, rows_ref)]
    small = [
        pltpu.make_async_copy(there, here, sems.at[2 * slots + n])
        for n, (there, here) in enumerate(pairs)
    ]
    for load in small + loads:
        load.start()
    for load in small:
        load.wait()
    for s in range(slots):
        request = jnp.maximum(owner_ref[0, s], 0)
        begin = len_ref[request] - owner_ref[1, s] * piece_rows
        start = pl.multiple_of(jnp.clip(begin, 0, piece_rows - span) // 16 * 16, 16)
        count = jnp.int32(0)
        for j in range(path_ref.shape[0]):
            count = count + (path_ref[j, request] >= 0).astype(jnp.int32)
        count = jnp.where(owner_ref[0, s] >= 0, count, 0)
        offset = iota((span, 16), 0) + (start - begin)
        lane = iota((span, 16), 1) - 12
        low = ((offset == lane) & (lane >= 0)).astype(jnp.bfloat16)
        high = ((offset == lane + 4) & (lane >= 0)).astype(jnp.bfloat16)
        chosen = jnp.dot(
            low, rows_ref[s, :, :width], preferred_element_type=jnp.float32
        ) + jnp.dot(high, rows_ref[s, :, width:], preferred_element_type=jnp.float32)
        offset = iota((span, width), 0) + (start - begin)
        writing = (offset >= 0) & (offset < count)
        loads[s].wait()
        near = held[s][pl.ds(start, span), :].astype(jnp.float32)
        held[s][pl.ds(start, span), :] = jnp.where(writing, chosen, near).astype(jnp.bfloat16)
        stores[s].start()
    for store in stores:
        store.wait()


def shards_grid(
    queries, tree_kv, tree_parent, accepted_path, cache_kv, piece_owner, cache_len, out_weight
):
    slots, piece_rows, width = cache_kv.shape
    tree_size = queries.shape[1]
    columns = queries.shape[2]
    reqs = 16
    half = reqs * tree_size // 2
    vmem = pl.BlockSpec(memory_space=pltpu.VMEM)
    hbm = pl.BlockSpec(memory_space=pltpu.HBM)
    pieces = reqs * (slots + 1)
    dma = pltpu.SemaphoreType.DMA
    bf16, f32, i32 = jnp.bfloat16, jnp.float32, jnp.int32
    owner_t, path_t = piece_owner.T, accepted_path.T
    mixed, rows = pl.pallas_call(
        layer_kernel,
        out_shape=(
            jax.ShapeDtypeStruct((half, out_weight.shape[1]), bf16),
            jax.ShapeDtypeStruct((slots, 16, columns), bf16),
        ),
        in_specs=[hbm] * 8,
        out_specs=(vmem, vmem),
        scratch_shapes=[
            pltpu.SMEM(owner_t.shape, i32),
            pltpu.VMEM(owner_t.shape, i32),
            pltpu.SMEM(cache_len.shape, i32),
            pltpu.VMEM(tree_parent.shape, i32),
            pltpu.VMEM(path_t.shape, i32),
            pltpu.VMEM(queries.shape, bf16),
            pltpu.VMEM(tree_kv.shape, bf16),
            pltpu.VMEM(cache_kv.shape, bf16),
            pltpu.VMEM(out_weight.shape, bf16),
            pltpu.VMEM((reqs, PAD, HD), bf16),
            pltpu.VMEM((reqs, PAD, HD), bf16),
            pltpu.VMEM((reqs, 8, 128), i32),
            pltpu.SMEM((reqs, 8, 128), i32),
            pltpu.VMEM((reqs - 1, slots * PAD, HD), bf16),
            pltpu.VMEM((reqs, slots * PAD, HD), bf16),
            pltpu.VMEM((PAD, columns), f32),
            pltpu.VMEM((PAD, width), f32),
            pltpu.VMEM((PAD, width), bf16),
            pltpu.VMEM((PAD, PAD), f32),
            pltpu.VMEM((4, 4, (slots + 1) * PAD, HD), bf16),
            pltpu.VMEM((reqs, (slots + 1) * PAD, HD), bf16),
            pltpu.VMEM((pieces * PAD, HD), f32),
            pltpu.VMEM((pieces, HD), f32),
            pltpu.VMEM((reqs // 2, PAD, HD), f32),
            pltpu.VMEM((half, HD), f32),
            pltpu.VMEM((2, reqs, half, HD), bf16),
            pltpu.VMEM((half, out_weight.shape[1]), bf16),
            pltpu.VMEM((half, out_weight.shape[1]), bf16),
            dma((10,)),
            dma((reqs,)),
            dma((reqs,)),
            dma((reqs,)),
            dma((reqs,)),
            dma((reqs,)),
            dma((reqs,)),
            dma((4, 4)),
            dma((reqs,)),
            dma((2, KINDS)),
            dma((2, KINDS)),
            dma,
            dma,
        ],
        compiler_params=pltpu.CompilerParams(
            collective_id=0, has_side_effects=True, vmem_limit_bytes=VMEM_LIMIT
        ),
    )(owner_t, cache_len, tree_parent, path_t, queries, tree_kv, cache_kv, out_weight)
    cache_out = pl.pallas_call(
        append_kernel,
        out_shape=jax.ShapeDtypeStruct(cache_kv.shape, bf16),
        in_specs=[hbm] * 5,
        out_specs=hbm,
        scratch_shapes=[
            pltpu.SMEM(owner_t.shape, i32),
            pltpu.SMEM(cache_len.shape, i32),
            pltpu.SMEM(path_t.shape, i32),
            pltpu.VMEM((slots, 16, columns), bf16),
            dma((2 * slots + 4,)),
        ]
        + [pltpu.VMEM(cache_kv.shape[1:], bf16)] * slots,
        compiler_params=pltpu.CompilerParams(vmem_limit_bytes=VMEM_LIMIT),
    )(owner_t, cache_len, path_t, cache_kv, rows)
    mixed = mixed.reshape(tree_size, reqs // 2, out_weight.shape[1]).transpose(1, 0, 2)
    return mixed, cache_out


def solution(mesh):
    body = shards_grid if dict(mesh.shape) == {"req": 16, "tp": 2} else shards_general
    return jax.shard_map(
        body,
        mesh=mesh,
        in_specs=(
            P("req", None, "tp"),
            P("req", None, "tp"),
            P("req", None),
            P(),
            P("req", None, "tp"),
            P("req", None),
            P(),
            P("tp", "req"),
        ),
        out_specs=(P("tp", None, "req"), P("req", None, "tp")),
        check_vma=False,
    )
```

```python
import math

import jax
import jax.numpy as jnp
from jax import lax
from jax.experimental import pallas as pl
from jax.experimental.pallas import tpu as pltpu
from jax.sharding import PartitionSpec as P

HD = 128


NEG = -1e30


def ancestors(parent):
    tree_size = parent.shape[-1]
    node_ids = lax.broadcasted_iota(jnp.int32, (tree_size, tree_size), 1)
    parent_hot = (parent[..., :, None] == node_ids).astype(jnp.float32)
    reached = jnp.minimum(parent_hot + jnp.eye(tree_size, dtype=jnp.float32), 1.0)
    for rounds in range(max(1, (tree_size - 1).bit_length())):
        reached = jnp.minimum(
            jnp.einsum("rij,rjk->rik", reached, reached, precision=lax.Precision.HIGHEST), 1.0
        )
    return reached


def shards_general(
    queries, tree_kv, tree_parent, accepted_path, cache_kv, piece_owner, cache_len, out_weight
):
    kvheads_local = tree_kv.shape[-1] // (2 * HD)
    heads_local = queries.shape[-1] // HD
    group_size = heads_local // kvheads_local
    tree_size = queries.shape[1]
    slot_count = cache_kv.shape[0]
    piece_rows = cache_kv.shape[1]
    depth_most = accepted_path.shape[1]
    scaling = 1.0 / math.sqrt(HD)
    every_query = lax.all_gather(queries, "req", axis=0, tiled=True)
    req_total = every_query.shape[0]
    owner_req = piece_owner[:, 0]
    owner_piece = piece_owner[:, 1]
    safe_req = jnp.maximum(owner_req, 0)
    slot_query = every_query[safe_req].reshape(slot_count, tree_size, kvheads_local, group_size, HD)
    stored = cache_kv.reshape(slot_count, piece_rows, kvheads_local, 2, HD)
    row_pos = owner_piece[:, None] * piece_rows + lax.broadcasted_iota(
        jnp.int32, (slot_count, piece_rows), 1
    )
    visible = (owner_req >= 0)[:, None] & (row_pos < cache_len[safe_req][:, None])
    wide_mask = visible[:, None, None, None, :]
    scores = (
        jnp.einsum(
            "stkgd,spkd->stkgp", slot_query, stored[:, :, :, 0], preferred_element_type=jnp.float32
        )
        * scaling
    )
    scores = jnp.where(wide_mask, scores, NEG)
    slot_peak = jnp.max(scores, -1)
    expo = jnp.where(wide_mask, jnp.exp(scores - slot_peak[..., None]), 0.0)
    slot_den = jnp.sum(expo, -1)
    weights = expo.astype(jnp.bfloat16)
    slot_num = jnp.einsum(
        "stkgp,spkd->stkgd", weights, stored[:, :, :, 1], preferred_element_type=jnp.float32
    )
    request_ids = lax.broadcasted_iota(jnp.int32, (req_total, slot_count), 0)
    member = (owner_req[None, :] == request_ids)[:, :, None, None, None]
    req_peak = jnp.max(jnp.where(member, slot_peak[None], NEG), axis=1)
    factor = jnp.where(
        member, jnp.exp(jnp.where(member, slot_peak[None] - req_peak[:, None], 0.0)), 0.0
    )
    req_den = jnp.sum(factor * slot_den[None], axis=1)
    req_num = jnp.einsum("rstkg,stkgd->rtkgd", factor, slot_num, precision=lax.Precision.HIGHEST)
    peak_table = req_peak.reshape(req_total, tree_size, heads_local)
    den_table = req_den.reshape(req_total, tree_size, heads_local)
    num_table = req_num.reshape(req_total, tree_size, heads_local * HD)
    own_index = lax.axis_index("req")
    got_peak, got_den, got_num = (
        lax.all_to_all(
            peak_table.astype(jnp.bfloat16), "req", split_axis=0, concat_axis=0, tiled=True
        ).astype(peak_table.dtype),
        lax.all_to_all(
            den_table.astype(jnp.bfloat16), "req", split_axis=0, concat_axis=0, tiled=True
        ).astype(den_table.dtype),
        lax.all_to_all(
            num_table.astype(jnp.bfloat16), "req", split_axis=0, concat_axis=0, tiled=True
        ).astype(num_table.dtype),
    )
    cache_peak = jnp.max(got_peak, axis=0)
    source_scale = jnp.exp(got_peak - cache_peak[None])
    cache_den = jnp.sum(source_scale * got_den, axis=0)
    got_rows = got_num.reshape(got_num.shape[0], tree_size, heads_local, HD)
    cache_num = jnp.sum(source_scale[..., None] * got_rows, axis=0)
    reached = ancestors(tree_parent)[0]
    home_query = queries[0].reshape(tree_size, kvheads_local, group_size, HD)
    fresh = tree_kv[0].reshape(tree_size, kvheads_local, 2, HD)
    tree_mask = reached[:, None, None, :] > 0.5
    tree_scores = (
        jnp.einsum("ikgd,jkd->ikgj", home_query, fresh[:, :, 0], preferred_element_type=jnp.float32)
        * scaling
    )
    tree_scores = jnp.where(tree_mask, tree_scores, NEG)
    tree_peak = jnp.max(tree_scores, -1)
    tree_exp = jnp.where(tree_mask, jnp.exp(tree_scores - tree_peak[..., None]), 0.0)
    tree_den = jnp.sum(tree_exp, -1).reshape(tree_size, heads_local)
    tree_num = jnp.einsum(
        "ikgj,jkd->ikgd",
        tree_exp.astype(jnp.bfloat16),
        fresh[:, :, 1],
        preferred_element_type=jnp.float32,
    )
    tree_num = tree_num.reshape(tree_size, heads_local, HD)
    tree_peak = tree_peak.reshape(tree_size, heads_local)
    total_peak = jnp.maximum(cache_peak, tree_peak)
    cache_scale = jnp.exp(cache_peak - total_peak)
    tree_scale = jnp.exp(tree_peak - total_peak)
    denom = cache_den * cache_scale + tree_den * tree_scale
    numer = cache_num * cache_scale[..., None] + tree_num * tree_scale[..., None]
    attention = (
        (numer / denom[..., None]).reshape(1, tree_size, heads_local * HD).astype(jnp.bfloat16)
    )
    piece = lax.all_gather(attention, "req", axis=0, tiled=True)
    flat_rows = piece.reshape(piece.shape[0] * piece.shape[1], piece.shape[2])
    product = jnp.dot(flat_rows, out_weight, preferred_element_type=jnp.float32)
    terms = product.reshape(piece.shape[0], piece.shape[1], out_weight.shape[1])
    mixed = lax.psum_scatter(terms.astype(jnp.bfloat16), "tp", scatter_dimension=0, tiled=True)
    own_path = lax.dynamic_index_in_dim(accepted_path, own_index, 0, keepdims=False)
    picked = tree_kv[0][jnp.maximum(own_path, 0)]
    picked = jnp.where((own_path >= 0)[:, None], picked, jnp.zeros_like(picked))
    all_rows = lax.all_gather(picked[None], "req", axis=0, tiled=True)
    counts = jnp.sum((accepted_path >= 0).astype(jnp.int32), axis=1)
    offset = row_pos - cache_len[safe_req][:, None]
    writing = (owner_req >= 0)[:, None] & (offset >= 0) & (offset < counts[safe_req][:, None])
    slot_rows = all_rows[safe_req]
    chosen = jnp.take_along_axis(slot_rows, jnp.clip(offset, 0, depth_most - 1)[:, :, None], axis=1)
    cache_out = jnp.where(writing[:, :, None], chosen, cache_kv)
    return (mixed, cache_out)


MESH = pl.DeviceIdType.MESH
PAD = 32
KINDS = 21
VMEM_LIMIT = 63 * 1024 * 1024


def place():
    me = lax.axis_index("req")
    z, y, x = me // 4, (me // 2) % 2, me % 2
    planes = [z, z + 1 - 2 * (z % 2), (z + 2) % 4, 3 - z]
    return me, y, x, planes


def arrivals():
    z = lax.axis_index("req") // 4
    return [z, z + 1 - 2 * (z % 2), 2 - z // 2, 3 - 3 * (z // 2)]


class GridGather:
    def __init__(self, buf, send, recv, part):
        me, y, x, planes = place()
        self.buf, self.send, self.recv, self.part = buf, send, recv, part
        self.column = [plane * 4 + y * 2 + x for plane in arrivals()]
        z = me // 4
        self.inner = (z + 1) // 2 == 1
        self.middle = (3 - z) * 4 + y * 2 + x
        self.to_x, self.to_y = 1 - 2 * x, 2 - 4 * y
        self.near_x, self.near_y = me + self.to_x, me + self.to_y
        self.me = me
        self.sent = []

    def copy(self, origin, piece, target, kind, arrive=None):
        rows = self.buf.shape[1]
        half = rows // 2
        start, size = {"all": (0, rows), "top": (0, half), "low": (half, half)}[piece]
        block = self.buf.at[origin, pl.ds(start, size)]
        return pltpu.make_async_remote_copy(
            src_ref=block,
            dst_ref=block,
            send_sem=self.send.at[self.part, kind],
            recv_sem=self.recv.at[self.part, kind if arrive is None else arrive],
            device_id={"req": target},
            device_id_type=MESH,
        )

    def go(self, *args):
        moving = self.copy(*args)
        moving.start()
        self.sent.append((None, moving))

    def relay(self, *args):
        @pl.when(self.inner)
        def _():
            self.copy(*args).start()

        self.sent.append((self.inner, args))

    def begin(self):
        self.go(self.me, "all", self.column[1], 0, 0)
        self.relay(self.me, "all", self.middle, 1, 1)
        self.step(0)

    def step(self, k):
        column = self.column
        if k < 4:
            if k:
                self.copy(column[k], "all", self.near_x, k - 1).wait_recv()
                if k == 1:
                    self.relay(column[1], "all", self.middle, 2, 2)
                else:
                    self.relay(column[k], "all", column[1], k + 1, k - 1)
            self.go(column[k], "all", self.near_x, 5 + k)
            self.go(column[k], "all", self.near_y, 9 + k)
        if k:
            across_x, across_y = column[k - 1] + self.to_x, column[k - 1] + self.to_y
            self.copy(across_x, "all", self.near_x, 4 + k).wait_recv()
            self.go(across_x, "top", self.near_y, 12 + k)
            self.copy(across_y, "all", self.near_x, 8 + k).wait_recv()
            self.go(across_y, "low", self.near_x, 16 + k)

    def end(self):
        for k in range(4):
            across = self.column[k] + self.to_x + self.to_y
            self.copy(across, "top", self.near_x, 13 + k).wait_recv()
            self.copy(across, "low", self.near_x, 17 + k).wait_recv()

    def finish(self):
        for only, moving in self.sent:
            if only is None:
                moving.wait_send()
                continue

            @pl.when(only)
            def _():
                self.copy(*moving).wait_send()


def iota(shape, dim):
    return lax.broadcasted_iota(jnp.int32, shape, dim)


def as_column(row):
    size = row.shape[1]
    shape = (size, size)
    return jnp.sum(
        jnp.where(iota(shape, 0) == iota(shape, 1), row, 0.0), axis=1, keepdims=True
    )


def attend(query, key, value, mask, scaling, owner):
    rows = query.shape[0]
    scores = scaling * lax.dot_general(
        query, key, (((1,), (1,)), ((), ())), preferred_element_type=jnp.float32
    )
    scores = jnp.where(mask, scores, NEG)
    peak = jnp.max(scores, axis=1, keepdims=True)
    expo = jnp.where(mask, jnp.exp(scores - peak), 0.0)
    denom = jnp.sum(expo, axis=1, keepdims=True)
    numer = jnp.dot(expo.astype(jnp.bfloat16), value, preferred_element_type=jnp.float32)
    some = denom > 0.0
    safe = jnp.where(some, denom, 1.0)
    level = jnp.where(some, peak + jnp.log(safe), NEG)
    out = numer * (1.0 / safe)
    shape = (PAD, HD)
    pick = iota(shape, 0) == iota(shape, 1)
    where = iota(shape, 0)
    blocks = []
    for g in range(rows // PAD):
        line = jnp.sum(
            jnp.where(pick, level[g * PAD : (g + 1) * PAD], 0.0), axis=0, keepdims=True
        )
        high = line.astype(jnp.bfloat16).astype(jnp.float32)
        block = out[g * PAD : (g + 1) * PAD]
        block = jnp.where(where == 28, high, block)
        block = jnp.where(where == 29, line - high, block)
        block = jnp.where(where == 30, owner, block)
        blocks.append(block.astype(jnp.bfloat16))
    return blocks


def layer_kernel(
    owner_h, len_h, parent_h, path_h, query_h, tree_h, cache_h, weight_h,
    mixed_ref, rows_ref,
    owner_ref, owner_v, len_ref, parent_ref, path_ref, query_ref, tree_ref, cache_v, weight_v,
    own_heads, owned, known_v, known, staged, asked, packed, tree_f, tree_b, reach_v, outgoing, incoming, tree_out, tree_in,
    wide, owners, joined, compact, attn, half_out, half_in,
    local_sem, send0, recv0, send5, recv5, send6, recv6, send1, recv1, send2, recv2, send3, recv3, send4, recv4,
):
    me, y, x, planes = place()
    tp = lax.axis_index("tp")
    tree_size = query_h.shape[1]
    slots = cache_h.shape[0]
    piece_rows = cache_h.shape[1]
    scaling = 1.0 / math.sqrt(HD)
    pairs = [
        (query_h, query_ref), (tree_h, tree_ref), (path_h, path_ref), (parent_h, parent_ref),
        (owner_h, owner_ref), (len_h, len_ref), (cache_h, cache_v), (weight_h, weight_v),
        (owner_h, owner_v),
    ]
    loads = [
        pltpu.make_async_copy(there, here, local_sem.at[n])
        for n, (there, here) in enumerate(pairs)
    ]
    for load in loads:
        load.start()

    barrier = pltpu.get_barrier_semaphore()
    for d in range(1, 16):
        pl.semaphore_signal(
            barrier, inc=1, device_id={"req": (me + d) % 16}, device_id_type=MESH
        )
    pl.semaphore_signal(barrier, inc=1, device_id={"tp": 1 - tp}, device_id_type=MESH)

    for load in loads[:3] + loads[8:9]:
        load.wait()
    tree_f[...] = jnp.zeros_like(tree_f)
    tree_f[0:tree_size] = tree_ref[0].astype(jnp.float32)
    tree_b[...] = tree_f[...].astype(jnp.bfloat16)
    table = path_ref[...].astype(jnp.float32)
    path = jnp.sum(jnp.where(iota(table.shape, 1) == me, table, 0.0), axis=1, keepdims=True)
    depth = path.shape[0]
    chosen = (path == iota((depth, PAD), 1).astype(jnp.float32)).astype(jnp.bfloat16)
    picked = jnp.dot(chosen, tree_b[...], preferred_element_type=jnp.float32)
    width = tree_h.shape[2]
    packed[0:tree_size] = query_ref[0].astype(jnp.float32)
    packed[tree_size:PAD, 0:width] = picked[0:4]
    packed[tree_size:PAD, width : 2 * width] = picked[4:8]
    for head in range(16):
        device = 4 * (head % 4) + head // 4
        own_heads[device] = packed[:, head * HD : (head + 1) * HD].astype(jnp.bfloat16)
    owned[me] = own_heads[me]
    known_v[me] = jnp.zeros(known_v.shape[1:], jnp.int32)
    known_v[me, 0:1, 0:slots] = owner_v[0:1, :]

    pl.semaphore_wait(barrier, 16)

    others = []
    for k in range(4):
        for c in range(4):
            others.append((planes[k] * 4 + (me + c) % 4, k + c > 0))
    others = [device for device, other in others if other]
    hops = []

    def post(block, to, target, send, recv, n):
        moving = pltpu.make_async_remote_copy(
            src_ref=block,
            dst_ref=to,
            send_sem=send.at[n],
            recv_sem=recv.at[me],
            device_id={"req": target},
            device_id_type=MESH,
        )
        moving.start()
        hops.append(moving)

    def take(block, send, recv, source):
        pltpu.make_async_remote_copy(
            src_ref=block,
            dst_ref=block,
            send_sem=send.at[0],
            recv_sem=recv.at[source],
            device_id={"req": (me + 1) % 16},
            device_id_type=MESH,
        ).wait_recv()

    for n, target in enumerate(others):
        post(known_v.at[me], known_v.at[me], target, send0, recv0, n)
    for n, target in enumerate(others):
        post(own_heads.at[target], owned.at[me], target, send1, recv1, n)

    loads[3].wait()
    parent = as_column(parent_ref[...].astype(jnp.float32))
    lanes = iota((tree_size, PAD), 1).astype(jnp.float32)
    reach_v[...] = (iota((PAD, PAD), 0) == iota((PAD, PAD), 1)).astype(jnp.float32)
    reach_v[0:tree_size] = jnp.minimum(
        reach_v[0:tree_size] + (parent == lanes).astype(jnp.float32), 1.0
    )
    reached = reach_v[...]
    for rounds in range(max(1, (tree_size - 1).bit_length())):
        short = reached.astype(jnp.bfloat16)
        reached = jnp.minimum(jnp.dot(short, short, preferred_element_type=jnp.float32), 1.0)
    tree_mask = jnp.concatenate([reached] * 4, axis=0) > 0.5
    for kv in range(4):
        query = jnp.concatenate([own_heads[4 * g + kv] for g in range(4)], axis=0)
        at = kv * 2 * HD
        blocks = attend(
            query, tree_b[:, at : at + HD], tree_b[:, at + HD : at + 2 * HD], tree_mask, scaling,
            me.astype(jnp.float32),
        )
        for g in range(4):
            tree_out[4 * g + kv] = blocks[g]
    for load in loads[4:7]:
        load.wait()
    for source in others:
        take(known_v.at[source], send0, recv0, source)
    table = pltpu.make_async_copy(known_v, known, local_sem.at[9])
    table.start()
    table.wait()
    for source in others:
        take(owned.at[source], send1, recv1, source)

    def stage(device, to):
        for s in range(slots):
            request = jnp.maximum(known[device, 0, s], 0)
            to[s * PAD : (s + 1) * PAD] = owned[request]

    for n, target in enumerate(others):
        stage(target, staged.at[n])
        post(staged.at[n], asked.at[me], target, send5, recv5, n)
    stage(me, asked.at[me])
    for n, target in enumerate(others):
        post(tree_out.at[target], tree_in.at[me], target, send6, recv6, n)
    tree_in[me] = tree_out[me]

    sent = []

    def attend_head(kv):
        for g in range(4):
            source = 4 * g + kv

            @pl.when(source != me)
            def _():
                take(asked.at[source], send5, recv5, source)

        for s in range(slots):
            owner = owner_ref[0, s]
            request = jnp.maximum(owner, 0)
            limit = jnp.where(owner >= 0, len_ref[request] - owner_ref[1, s] * piece_rows, 0)
            mask = iota((4 * PAD, piece_rows), 1) < limit
            keys = cache_v.at[s]
            parts = [asked[4 * g + kv, s * PAD : (s + 1) * PAD, :] for g in range(4)]
            query = jnp.concatenate(parts, axis=0)
            at = kv * 2 * HD
            blocks = attend(
                query, keys[:, at : at + HD], keys[:, at + HD : at + 2 * HD], mask, scaling,
                owner.astype(jnp.float32),
            )
            for g in range(4):
                outgoing[kv, g, s * PAD : (s + 1) * PAD] = blocks[g]
        for k in range(4):
            plane = planes[k]
            target = plane * 4 + kv

            def remote(target=target, plane=plane, k=k):
                return pltpu.make_async_remote_copy(
                    src_ref=outgoing.at[kv, plane],
                    dst_ref=incoming.at[me],
                    send_sem=send2.at[kv, k],
                    recv_sem=recv2.at[me],
                    device_id={"req": target},
                    device_id_type=MESH,
                )

            if k == 0:

                @pl.when(target != me)
                def _():
                    remote().start()

                @pl.when(target == me)
                def _():
                    incoming[me] = outgoing[kv, plane]

            else:
                remote().start()
            sent.append((k, target, remote))

    for kv in range(4):
        attend_head(kv)
    for s in range(slots):
        for head in range(16):
            device = 4 * (head % 4) + head // 4
            rows_ref[s, :, head * HD : (head + 1) * HD] = asked[
                device, s * PAD + 16 : (s + 1) * PAD, :
            ]
    for d in range(1, 16):
        source = (me + d) % 16
        pltpu.make_async_remote_copy(
            src_ref=outgoing.at[0, 0],
            dst_ref=incoming.at[source],
            send_sem=send2.at[0, 0],
            recv_sem=recv2.at[source],
            device_id={"req": source},
            device_id_type=MESH,
        ).wait_recv()

    pieces = 16 * (slots + 1)
    for source in others:
        take(tree_in.at[source], send6, recv6, source)
    held = 16 * slots
    wide[0 : held * PAD] = incoming[...].astype(jnp.float32).reshape(held * PAD, HD)
    wide[held * PAD :] = tree_in[...].astype(jnp.float32).reshape(16 * PAD, HD)
    level = wide[pl.ds(28, pieces, stride=PAD), :] + wide[pl.ds(29, pieces, stride=PAD), :]
    holder = wide[pl.ds(30, pieces, stride=PAD), :]
    owners[...] = holder
    share = jnp.zeros_like(level)
    for r in range(16):
        member = holder == float(r)
        peak = jnp.max(jnp.where(member, level, NEG), axis=0, keepdims=True)
        expo = jnp.where(member, jnp.exp(jnp.where(member, level - peak, 0.0)), 0.0)
        share = share + expo * (1.0 / jnp.sum(expo, axis=0, keepdims=True))
    turned = share.T
    for b in range(pieces):
        block = slice(b * PAD, (b + 1) * PAD)
        wide[block] = wide[block] * turned[0:PAD, b : b + 1]

    def join_half(part, to):
        def join(i, carry):
            r = part * 8 + i
            mine = r.astype(jnp.float32)
            first_row = pl.multiple_of((held + r) * PAD, PAD)
            total = wide[pl.ds(first_row, PAD), :]
            for b in range(held):
                total = total + jnp.where(
                    owners[b : b + 1] == mine, wide[b * PAD : (b + 1) * PAD], 0.0
                )
            joined[i] = total
            return carry

        lax.fori_loop(0, 8, join, 0)
        for i in range(8):
            compact[pl.ds(i, tree_size, stride=8), :] = joined[i, 0:tree_size]
        attn[to, me] = compact[...].astype(jnp.bfloat16)

    last = [GridGather(attn.at[c], send3, recv3, c) for c in range(2)]
    join_half(1 - tp, 0)
    last[0].begin()
    join_half(tp, 1)
    last[0].step(1)
    last[1].begin()
    last[0].step(2)
    last[1].step(1)
    last[0].step(3)
    last[1].step(2)
    last[0].step(4)
    last[1].step(3)
    loads[7].wait()

    def project(part):
        total = jnp.zeros(half_out.shape, jnp.float32)
        for kv in range(4):
            for g in range(0, 4, 2):
                head = 4 * kv + g
                pair = jnp.concatenate(
                    [attn[part, 4 * g + kv], attn[part, 4 * g + 4 + kv]], axis=1
                )
                total = total + jnp.dot(
                    pair, weight_v[head * HD : (head + 2) * HD],
                    preferred_element_type=jnp.float32,
                )
        return total

    last[0].end()
    last[1].step(4)
    half_out[...] = project(0).astype(jnp.bfloat16)
    swap = pltpu.make_async_remote_copy(
        src_ref=half_out,
        dst_ref=half_in,
        send_sem=send4,
        recv_sem=recv4,
        device_id={"tp": 1 - tp},
        device_id_type=MESH,
    )
    swap.start()
    last[1].end()
    own_half = project(1)
    swap.wait_recv()
    mixed_ref[...] = (own_half + half_in[...].astype(jnp.float32)).astype(jnp.bfloat16)

    swap.wait_send()
    for hop in hops:
        hop.wait_send()
    for gather in last:
        gather.finish()
    for k, target, remote in sent:
        if k == 0:

            @pl.when(target != me)
            def _():
                remote().wait_send()

        else:
            remote().wait_send()


def append_kernel(
    owner_h, len_h, path_h, cache_ref, rows_h, out_ref,
    owner_ref, len_ref, path_ref, rows_ref, sems, *held,
):
    slots, piece_rows, width = cache_ref.shape
    span = 32
    loads = [pltpu.make_async_copy(cache_ref.at[s], held[s], sems.at[s]) for s in range(slots)]
    stores = [
        pltpu.make_async_copy(held[s], out_ref.at[s], sems.at[slots + s]) for s in range(slots)
    ]
    pairs = [(owner_h, owner_ref), (len_h, len_ref), (path_h, path_ref), (rows_h, rows_ref)]
    small = [
        pltpu.make_async_copy(there, here, sems.at[2 * slots + n])
        for n, (there, here) in enumerate(pairs)
    ]
    for load in small + loads:
        load.start()
    for load in small:
        load.wait()
    for s in range(slots):
        request = jnp.maximum(owner_ref[0, s], 0)
        begin = len_ref[request] - owner_ref[1, s] * piece_rows
        start = pl.multiple_of(jnp.clip(begin, 0, piece_rows - span) // 16 * 16, 16)
        count = jnp.int32(0)
        for j in range(path_ref.shape[0]):
            count = count + (path_ref[j, request] >= 0).astype(jnp.int32)
        count = jnp.where(owner_ref[0, s] >= 0, count, 0)
        offset = iota((span, 16), 0) + (start - begin)
        lane = iota((span, 16), 1) - 12
        low = ((offset == lane) & (lane >= 0)).astype(jnp.bfloat16)
        high = ((offset == lane + 4) & (lane >= 0)).astype(jnp.bfloat16)
        chosen = jnp.dot(
            low, rows_ref[s, :, :width], preferred_element_type=jnp.float32
        ) + jnp.dot(high, rows_ref[s, :, width:], preferred_element_type=jnp.float32)
        offset = iota((span, width), 0) + (start - begin)
        writing = (offset >= 0) & (offset < count)
        loads[s].wait()
        near = held[s][pl.ds(start, span), :].astype(jnp.float32)
        held[s][pl.ds(start, span), :] = jnp.where(writing, chosen, near).astype(jnp.bfloat16)
        stores[s].start()
    for store in stores:
        store.wait()


def shards_grid(
    queries, tree_kv, tree_parent, accepted_path, cache_kv, piece_owner, cache_len, out_weight
):
    slots, piece_rows, width = cache_kv.shape
    tree_size = queries.shape[1]
    columns = queries.shape[2]
    reqs = 16
    half = reqs * tree_size // 2
    vmem = pl.BlockSpec(memory_space=pltpu.VMEM)
    hbm = pl.BlockSpec(memory_space=pltpu.HBM)
    pieces = reqs * (slots + 1)
    dma = pltpu.SemaphoreType.DMA
    bf16, f32, i32 = jnp.bfloat16, jnp.float32, jnp.int32
    owner_t, path_t = piece_owner.T, accepted_path.T
    mixed, rows = pl.pallas_call(
        layer_kernel,
        out_shape=(
            jax.ShapeDtypeStruct((half, out_weight.shape[1]), bf16),
            jax.ShapeDtypeStruct((slots, 16, columns), bf16),
        ),
        in_specs=[hbm] * 8,
        out_specs=(vmem, vmem),
        scratch_shapes=[
            pltpu.SMEM(owner_t.shape, i32),
            pltpu.VMEM(owner_t.shape, i32),
            pltpu.SMEM(cache_len.shape, i32),
            pltpu.VMEM(tree_parent.shape, i32),
            pltpu.VMEM(path_t.shape, i32),
            pltpu.VMEM(queries.shape, bf16),
            pltpu.VMEM(tree_kv.shape, bf16),
            pltpu.VMEM(cache_kv.shape, bf16),
            pltpu.VMEM(out_weight.shape, bf16),
            pltpu.VMEM((reqs, PAD, HD), bf16),
            pltpu.VMEM((reqs, PAD, HD), bf16),
            pltpu.VMEM((reqs, 1, 128), i32),
            pltpu.SMEM((reqs, 1, 128), i32),
            pltpu.VMEM((reqs - 1, slots * PAD, HD), bf16),
            pltpu.VMEM((reqs, slots * PAD, HD), bf16),
            pltpu.VMEM((PAD, columns), f32),
            pltpu.VMEM((PAD, width), f32),
            pltpu.VMEM((PAD, width), bf16),
            pltpu.VMEM((PAD, PAD), f32),
            pltpu.VMEM((4, 4, slots * PAD, HD), bf16),
            pltpu.VMEM((reqs, slots * PAD, HD), bf16),
            pltpu.VMEM((reqs, PAD, HD), bf16),
            pltpu.VMEM((reqs, PAD, HD), bf16),
            pltpu.VMEM((pieces * PAD, HD), f32),
            pltpu.VMEM((pieces, HD), f32),
            pltpu.VMEM((reqs // 2, PAD, HD), f32),
            pltpu.VMEM((half, HD), f32),
            pltpu.VMEM((2, reqs, half, HD), bf16),
            pltpu.VMEM((half, out_weight.shape[1]), bf16),
            pltpu.VMEM((half, out_weight.shape[1]), bf16),
            dma((10,)),
            dma((reqs,)),
            dma((reqs,)),
            dma((reqs,)),
            dma((reqs,)),
            dma((reqs,)),
            dma((reqs,)),
            dma((reqs,)),
            dma((reqs,)),
            dma((4, 4)),
            dma((reqs,)),
            dma((2, KINDS)),
            dma((2, KINDS)),
            dma,
            dma,
        ],
        compiler_params=pltpu.CompilerParams(
            collective_id=0, has_side_effects=True, vmem_limit_bytes=VMEM_LIMIT
        ),
    )(owner_t, cache_len, tree_parent, path_t, queries, tree_kv, cache_kv, out_weight)
    cache_out = pl.pallas_call(
        append_kernel,
        out_shape=jax.ShapeDtypeStruct(cache_kv.shape, bf16),
        in_specs=[hbm] * 5,
        out_specs=hbm,
        scratch_shapes=[
            pltpu.SMEM(owner_t.shape, i32),
            pltpu.SMEM(cache_len.shape, i32),
            pltpu.SMEM(path_t.shape, i32),
            pltpu.VMEM((slots, 16, columns), bf16),
            dma((2 * slots + 4,)),
        ]
        + [pltpu.VMEM(cache_kv.shape[1:], bf16)] * slots,
        compiler_params=pltpu.CompilerParams(vmem_limit_bytes=VMEM_LIMIT),
    )(owner_t, cache_len, path_t, cache_kv, rows)
    mixed = mixed.reshape(tree_size, reqs // 2, out_weight.shape[1]).transpose(1, 0, 2)
    return mixed, cache_out


def solution(mesh):
    body = shards_grid if dict(mesh.shape) == {"req": 16, "tp": 2} else shards_general
    return jax.shard_map(
        body,
        mesh=mesh,
        in_specs=(
            P("req", None, "tp"),
            P("req", None, "tp"),
            P("req", None),
            P(),
            P("req", None, "tp"),
            P("req", None),
            P(),
            P("tp", "req"),
        ),
        out_specs=(P("tp", None, "req"), P("req", None, "tp")),
        check_vma=False,
    )
```

```python
import math

import jax
import jax.numpy as jnp
from jax import lax
from jax.experimental import pallas as pl
from jax.experimental.pallas import tpu as pltpu
from jax.sharding import PartitionSpec as P

HD = 128


NEG = -1e30


def ancestors(parent):
    tree_size = parent.shape[-1]
    node_ids = lax.broadcasted_iota(jnp.int32, (tree_size, tree_size), 1)
    parent_hot = (parent[..., :, None] == node_ids).astype(jnp.float32)
    reached = jnp.minimum(parent_hot + jnp.eye(tree_size, dtype=jnp.float32), 1.0)
    for rounds in range(max(1, (tree_size - 1).bit_length())):
        reached = jnp.minimum(
            jnp.einsum("rij,rjk->rik", reached, reached, precision=lax.Precision.HIGHEST), 1.0
        )
    return reached


def shards_general(
    queries, tree_kv, tree_parent, accepted_path, cache_kv, piece_owner, cache_len, out_weight
):
    kvheads_local = tree_kv.shape[-1] // (2 * HD)
    heads_local = queries.shape[-1] // HD
    group_size = heads_local // kvheads_local
    tree_size = queries.shape[1]
    slot_count = cache_kv.shape[0]
    piece_rows = cache_kv.shape[1]
    depth_most = accepted_path.shape[1]
    scaling = 1.0 / math.sqrt(HD)
    every_query = lax.all_gather(queries, "req", axis=0, tiled=True)
    req_total = every_query.shape[0]
    owner_req = piece_owner[:, 0]
    owner_piece = piece_owner[:, 1]
    safe_req = jnp.maximum(owner_req, 0)
    slot_query = every_query[safe_req].reshape(slot_count, tree_size, kvheads_local, group_size, HD)
    stored = cache_kv.reshape(slot_count, piece_rows, kvheads_local, 2, HD)
    row_pos = owner_piece[:, None] * piece_rows + lax.broadcasted_iota(
        jnp.int32, (slot_count, piece_rows), 1
    )
    visible = (owner_req >= 0)[:, None] & (row_pos < cache_len[safe_req][:, None])
    wide_mask = visible[:, None, None, None, :]
    scores = (
        jnp.einsum(
            "stkgd,spkd->stkgp", slot_query, stored[:, :, :, 0], preferred_element_type=jnp.float32
        )
        * scaling
    )
    scores = jnp.where(wide_mask, scores, NEG)
    slot_peak = jnp.max(scores, -1)
    expo = jnp.where(wide_mask, jnp.exp(scores - slot_peak[..., None]), 0.0)
    slot_den = jnp.sum(expo, -1)
    weights = expo.astype(jnp.bfloat16)
    slot_num = jnp.einsum(
        "stkgp,spkd->stkgd", weights, stored[:, :, :, 1], preferred_element_type=jnp.float32
    )
    request_ids = lax.broadcasted_iota(jnp.int32, (req_total, slot_count), 0)
    member = (owner_req[None, :] == request_ids)[:, :, None, None, None]
    req_peak = jnp.max(jnp.where(member, slot_peak[None], NEG), axis=1)
    factor = jnp.where(
        member, jnp.exp(jnp.where(member, slot_peak[None] - req_peak[:, None], 0.0)), 0.0
    )
    req_den = jnp.sum(factor * slot_den[None], axis=1)
    req_num = jnp.einsum("rstkg,stkgd->rtkgd", factor, slot_num, precision=lax.Precision.HIGHEST)
    peak_table = req_peak.reshape(req_total, tree_size, heads_local)
    den_table = req_den.reshape(req_total, tree_size, heads_local)
    num_table = req_num.reshape(req_total, tree_size, heads_local * HD)
    own_index = lax.axis_index("req")
    got_peak, got_den, got_num = (
        lax.all_to_all(
            peak_table.astype(jnp.bfloat16), "req", split_axis=0, concat_axis=0, tiled=True
        ).astype(peak_table.dtype),
        lax.all_to_all(
            den_table.astype(jnp.bfloat16), "req", split_axis=0, concat_axis=0, tiled=True
        ).astype(den_table.dtype),
        lax.all_to_all(
            num_table.astype(jnp.bfloat16), "req", split_axis=0, concat_axis=0, tiled=True
        ).astype(num_table.dtype),
    )
    cache_peak = jnp.max(got_peak, axis=0)
    source_scale = jnp.exp(got_peak - cache_peak[None])
    cache_den = jnp.sum(source_scale * got_den, axis=0)
    got_rows = got_num.reshape(got_num.shape[0], tree_size, heads_local, HD)
    cache_num = jnp.sum(source_scale[..., None] * got_rows, axis=0)
    reached = ancestors(tree_parent)[0]
    home_query = queries[0].reshape(tree_size, kvheads_local, group_size, HD)
    fresh = tree_kv[0].reshape(tree_size, kvheads_local, 2, HD)
    tree_mask = reached[:, None, None, :] > 0.5
    tree_scores = (
        jnp.einsum("ikgd,jkd->ikgj", home_query, fresh[:, :, 0], preferred_element_type=jnp.float32)
        * scaling
    )
    tree_scores = jnp.where(tree_mask, tree_scores, NEG)
    tree_peak = jnp.max(tree_scores, -1)
    tree_exp = jnp.where(tree_mask, jnp.exp(tree_scores - tree_peak[..., None]), 0.0)
    tree_den = jnp.sum(tree_exp, -1).reshape(tree_size, heads_local)
    tree_num = jnp.einsum(
        "ikgj,jkd->ikgd",
        tree_exp.astype(jnp.bfloat16),
        fresh[:, :, 1],
        preferred_element_type=jnp.float32,
    )
    tree_num = tree_num.reshape(tree_size, heads_local, HD)
    tree_peak = tree_peak.reshape(tree_size, heads_local)
    total_peak = jnp.maximum(cache_peak, tree_peak)
    cache_scale = jnp.exp(cache_peak - total_peak)
    tree_scale = jnp.exp(tree_peak - total_peak)
    denom = cache_den * cache_scale + tree_den * tree_scale
    numer = cache_num * cache_scale[..., None] + tree_num * tree_scale[..., None]
    attention = (
        (numer / denom[..., None]).reshape(1, tree_size, heads_local * HD).astype(jnp.bfloat16)
    )
    piece = lax.all_gather(attention, "req", axis=0, tiled=True)
    flat_rows = piece.reshape(piece.shape[0] * piece.shape[1], piece.shape[2])
    product = jnp.dot(flat_rows, out_weight, preferred_element_type=jnp.float32)
    terms = product.reshape(piece.shape[0], piece.shape[1], out_weight.shape[1])
    mixed = lax.psum_scatter(terms.astype(jnp.bfloat16), "tp", scatter_dimension=0, tiled=True)
    own_path = lax.dynamic_index_in_dim(accepted_path, own_index, 0, keepdims=False)
    picked = tree_kv[0][jnp.maximum(own_path, 0)]
    picked = jnp.where((own_path >= 0)[:, None], picked, jnp.zeros_like(picked))
    all_rows = lax.all_gather(picked[None], "req", axis=0, tiled=True)
    counts = jnp.sum((accepted_path >= 0).astype(jnp.int32), axis=1)
    offset = row_pos - cache_len[safe_req][:, None]
    writing = (owner_req >= 0)[:, None] & (offset >= 0) & (offset < counts[safe_req][:, None])
    slot_rows = all_rows[safe_req]
    chosen = jnp.take_along_axis(slot_rows, jnp.clip(offset, 0, depth_most - 1)[:, :, None], axis=1)
    cache_out = jnp.where(writing[:, :, None], chosen, cache_kv)
    return (mixed, cache_out)


MESH = pl.DeviceIdType.MESH
PAD = 32
KINDS = 21
VMEM_LIMIT = 63 * 1024 * 1024


def place():
    me = lax.axis_index("req")
    z, y, x = me // 4, (me // 2) % 2, me % 2
    planes = [z, z + 1 - 2 * (z % 2), (z + 2) % 4, 3 - z]
    return me, y, x, planes


def arrivals():
    z = lax.axis_index("req") // 4
    return [z, z + 1 - 2 * (z % 2), 2 - z // 2, 3 - 3 * (z // 2)]


class GridGather:
    def __init__(self, buf, send, recv, part):
        me, y, x, planes = place()
        self.buf, self.send, self.recv, self.part = buf, send, recv, part
        self.column = [plane * 4 + y * 2 + x for plane in arrivals()]
        z = me // 4
        self.inner = (z + 1) // 2 == 1
        self.middle = (3 - z) * 4 + y * 2 + x
        self.to_x, self.to_y = 1 - 2 * x, 2 - 4 * y
        self.near_x, self.near_y = me + self.to_x, me + self.to_y
        self.me = me
        self.sent = []

    def copy(self, origin, piece, target, kind, arrive=None):
        rows = self.buf.shape[1]
        half = rows // 2
        start, size = {"all": (0, rows), "top": (0, half), "low": (half, half)}[piece]
        block = self.buf.at[origin, pl.ds(start, size)]
        return pltpu.make_async_remote_copy(
            src_ref=block,
            dst_ref=block,
            send_sem=self.send.at[self.part, kind],
            recv_sem=self.recv.at[self.part, kind if arrive is None else arrive],
            device_id={"req": target},
            device_id_type=MESH,
        )

    def go(self, *args):
        moving = self.copy(*args)
        moving.start()
        self.sent.append((None, moving))

    def relay(self, *args):
        @pl.when(self.inner)
        def _():
            self.copy(*args).start()

        self.sent.append((self.inner, args))

    def begin(self):
        self.go(self.me, "all", self.column[1], 0, 0)
        self.relay(self.me, "all", self.middle, 1, 1)
        self.along(0)

    def along(self, k):
        column = self.column
        if k:
            self.copy(column[k], "all", self.near_x, k - 1).wait_recv()
            if k == 1:
                self.relay(column[1], "all", self.middle, 2, 2)
            else:
                self.relay(column[k], "all", column[1], k + 1, k - 1)
        self.go(column[k], "all", self.near_x, 5 + k)
        self.go(column[k], "all", self.near_y, 9 + k)

    def across(self, k):
        across_x, across_y = self.column[k] + self.to_x, self.column[k] + self.to_y
        self.copy(across_x, "all", self.near_x, 5 + k).wait_recv()
        self.go(across_x, "top", self.near_y, 13 + k)
        self.copy(across_y, "all", self.near_x, 9 + k).wait_recv()
        self.go(across_y, "low", self.near_x, 17 + k)

    def end(self):
        for k in range(4):
            across = self.column[k] + self.to_x + self.to_y
            self.copy(across, "top", self.near_x, 13 + k).wait_recv()
            self.copy(across, "low", self.near_x, 17 + k).wait_recv()

    def finish(self):
        for only, moving in self.sent:
            if only is None:
                moving.wait_send()
                continue

            @pl.when(only)
            def _():
                self.copy(*moving).wait_send()


def iota(shape, dim):
    return lax.broadcasted_iota(jnp.int32, shape, dim)


def as_column(row):
    size = row.shape[1]
    shape = (size, size)
    return jnp.sum(
        jnp.where(iota(shape, 0) == iota(shape, 1), row, 0.0), axis=1, keepdims=True
    )


def attend(query, key, value, mask, scaling, owner):
    rows = query.shape[0]
    scores = scaling * lax.dot_general(
        query, key, (((1,), (1,)), ((), ())), preferred_element_type=jnp.float32
    )
    scores = jnp.where(mask, scores, NEG)
    peak = jnp.max(scores, axis=1, keepdims=True)
    expo = jnp.where(mask, jnp.exp(scores - peak), 0.0)
    denom = jnp.sum(expo, axis=1, keepdims=True)
    numer = jnp.dot(expo.astype(jnp.bfloat16), value, preferred_element_type=jnp.float32)
    some = denom > 0.0
    safe = jnp.where(some, denom, 1.0)
    level = jnp.where(some, peak + jnp.log(safe), NEG)
    out = numer * (1.0 / safe)
    shape = (PAD, HD)
    pick = iota(shape, 0) == iota(shape, 1)
    where = iota(shape, 0)
    blocks = []
    for g in range(rows // PAD):
        line = jnp.sum(
            jnp.where(pick, level[g * PAD : (g + 1) * PAD], 0.0), axis=0, keepdims=True
        )
        high = line.astype(jnp.bfloat16).astype(jnp.float32)
        block = out[g * PAD : (g + 1) * PAD]
        block = jnp.where(where == 28, high, block)
        block = jnp.where(where == 29, line - high, block)
        block = jnp.where(where == 30, owner, block)
        blocks.append(block.astype(jnp.bfloat16))
    return blocks


def layer_kernel(
    owner_h, len_h, parent_h, path_h, query_h, tree_h, cache_h, weight_h,
    mixed_ref, rows_ref,
    owner_ref, owner_v, len_ref, parent_ref, path_ref, query_ref, tree_ref, cache_v, weight_v,
    own_heads, owned, known_v, known, staged, asked, packed, tree_f, tree_b, reach_v, outgoing, incoming, tree_out, tree_in,
    wide, owners, joined, compact, attn, half_out, half_in,
    local_sem, send0, recv0, send5, recv5, send6, recv6, send1, recv1, send2, recv2, send3, recv3, send4, recv4,
):
    me, y, x, planes = place()
    tp = lax.axis_index("tp")
    tree_size = query_h.shape[1]
    slots = cache_h.shape[0]
    piece_rows = cache_h.shape[1]
    scaling = 1.0 / math.sqrt(HD)
    pairs = [
        (query_h, query_ref), (tree_h, tree_ref), (path_h, path_ref), (parent_h, parent_ref),
        (owner_h, owner_ref), (len_h, len_ref), (cache_h, cache_v), (weight_h, weight_v),
        (owner_h, owner_v),
    ]
    loads = [
        pltpu.make_async_copy(there, here, local_sem.at[n])
        for n, (there, here) in enumerate(pairs)
    ]
    for load in loads:
        load.start()

    barrier = pltpu.get_barrier_semaphore()
    for d in range(1, 16):
        pl.semaphore_signal(
            barrier, inc=1, device_id={"req": (me + d) % 16}, device_id_type=MESH
        )
    pl.semaphore_signal(barrier, inc=1, device_id={"tp": 1 - tp}, device_id_type=MESH)

    for load in loads[:3] + loads[8:9]:
        load.wait()
    tree_f[...] = jnp.zeros_like(tree_f)
    tree_f[0:tree_size] = tree_ref[0].astype(jnp.float32)
    tree_b[...] = tree_f[...].astype(jnp.bfloat16)
    table = path_ref[...].astype(jnp.float32)
    path = jnp.sum(jnp.where(iota(table.shape, 1) == me, table, 0.0), axis=1, keepdims=True)
    depth = path.shape[0]
    chosen = (path == iota((depth, PAD), 1).astype(jnp.float32)).astype(jnp.bfloat16)
    picked = jnp.dot(chosen, tree_b[...], preferred_element_type=jnp.float32)
    width = tree_h.shape[2]
    packed[0:tree_size] = query_ref[0].astype(jnp.float32)
    packed[tree_size:PAD, 0:width] = picked[0:4]
    packed[tree_size:PAD, width : 2 * width] = picked[4:8]
    for head in range(16):
        device = 4 * (head % 4) + head // 4
        own_heads[device] = packed[:, head * HD : (head + 1) * HD].astype(jnp.bfloat16)
    owned[me] = own_heads[me]
    known_v[me] = jnp.zeros(known_v.shape[1:], jnp.int32)
    known_v[me, 0:1, 0:slots] = owner_v[0:1, :]

    pl.semaphore_wait(barrier, 16)

    others = []
    for k in range(4):
        for c in range(4):
            others.append((planes[k] * 4 + (me + c) % 4, k + c > 0))
    others = [device for device, other in others if other]
    hops = []

    def post(block, to, target, send, recv, n):
        moving = pltpu.make_async_remote_copy(
            src_ref=block,
            dst_ref=to,
            send_sem=send.at[n],
            recv_sem=recv.at[me],
            device_id={"req": target},
            device_id_type=MESH,
        )
        moving.start()
        hops.append(moving)

    def take(block, send, recv, source):
        pltpu.make_async_remote_copy(
            src_ref=block,
            dst_ref=block,
            send_sem=send.at[0],
            recv_sem=recv.at[source],
            device_id={"req": (me + 1) % 16},
            device_id_type=MESH,
        ).wait_recv()

    for n, target in enumerate(others):
        post(known_v.at[me], known_v.at[me], target, send0, recv0, n)
    for n, target in enumerate(others):
        post(own_heads.at[target], owned.at[me], target, send1, recv1, n)

    loads[3].wait()
    parent = as_column(parent_ref[...].astype(jnp.float32))
    lanes = iota((tree_size, PAD), 1).astype(jnp.float32)
    reach_v[...] = (iota((PAD, PAD), 0) == iota((PAD, PAD), 1)).astype(jnp.float32)
    reach_v[0:tree_size] = jnp.minimum(
        reach_v[0:tree_size] + (parent == lanes).astype(jnp.float32), 1.0
    )
    reached = reach_v[...]
    for rounds in range(max(1, (tree_size - 1).bit_length())):
        short = reached.astype(jnp.bfloat16)
        reached = jnp.minimum(jnp.dot(short, short, preferred_element_type=jnp.float32), 1.0)
    tree_mask = jnp.concatenate([reached] * 4, axis=0) > 0.5
    for kv in range(4):
        query = jnp.concatenate([own_heads[4 * g + kv] for g in range(4)], axis=0)
        at = kv * 2 * HD
        blocks = attend(
            query, tree_b[:, at : at + HD], tree_b[:, at + HD : at + 2 * HD], tree_mask, scaling,
            me.astype(jnp.float32),
        )
        for g in range(4):
            tree_out[4 * g + kv] = blocks[g]
    for load in loads[4:7]:
        load.wait()
    for source in others:
        take(known_v.at[source], send0, recv0, source)
    table = pltpu.make_async_copy(known_v, known, local_sem.at[9])
    table.start()
    table.wait()
    for source in others:
        take(owned.at[source], send1, recv1, source)

    def stage(device, to):
        for s in range(slots):
            request = jnp.maximum(known[device, 0, s], 0)
            to[s * PAD : (s + 1) * PAD] = owned[request]

    for n, target in enumerate(others):
        stage(target, staged.at[n])
        post(staged.at[n], asked.at[me], target, send5, recv5, n)
    stage(me, asked.at[me])
    for n, target in enumerate(others):
        post(tree_out.at[target], tree_in.at[me], target, send6, recv6, n)
    tree_in[me] = tree_out[me]

    sent = []

    def attend_head(kv):
        for g in range(4):
            source = 4 * g + kv

            @pl.when(source != me)
            def _():
                take(asked.at[source], send5, recv5, source)

        for s in range(slots):
            owner = owner_ref[0, s]
            request = jnp.maximum(owner, 0)
            limit = jnp.where(owner >= 0, len_ref[request] - owner_ref[1, s] * piece_rows, 0)
            mask = iota((4 * PAD, piece_rows), 1) < limit
            keys = cache_v.at[s]
            parts = [asked[4 * g + kv, s * PAD : (s + 1) * PAD, :] for g in range(4)]
            query = jnp.concatenate(parts, axis=0)
            at = kv * 2 * HD
            blocks = attend(
                query, keys[:, at : at + HD], keys[:, at + HD : at + 2 * HD], mask, scaling,
                owner.astype(jnp.float32),
            )
            for g in range(4):
                outgoing[kv, g, s * PAD : (s + 1) * PAD] = blocks[g]
        for k in range(4):
            plane = planes[k]
            target = plane * 4 + kv

            def remote(target=target, plane=plane, k=k):
                return pltpu.make_async_remote_copy(
                    src_ref=outgoing.at[kv, plane],
                    dst_ref=incoming.at[me],
                    send_sem=send2.at[kv, k],
                    recv_sem=recv2.at[me],
                    device_id={"req": target},
                    device_id_type=MESH,
                )

            if k == 0:

                @pl.when(target != me)
                def _():
                    remote().start()

                @pl.when(target == me)
                def _():
                    incoming[me] = outgoing[kv, plane]

            else:
                remote().start()
            sent.append((k, target, remote))

    for kv in range(4):
        attend_head(kv)
    for s in range(slots):
        for head in range(16):
            device = 4 * (head % 4) + head // 4
            rows_ref[s, :, head * HD : (head + 1) * HD] = asked[
                device, s * PAD + 16 : (s + 1) * PAD, :
            ]
    for d in range(1, 16):
        source = (me + d) % 16
        pltpu.make_async_remote_copy(
            src_ref=outgoing.at[0, 0],
            dst_ref=incoming.at[source],
            send_sem=send2.at[0, 0],
            recv_sem=recv2.at[source],
            device_id={"req": source},
            device_id_type=MESH,
        ).wait_recv()

    pieces = 16 * (slots + 1)
    for source in others:
        take(tree_in.at[source], send6, recv6, source)
    held = 16 * slots
    wide[0 : held * PAD] = incoming[...].astype(jnp.float32).reshape(held * PAD, HD)
    wide[held * PAD :] = tree_in[...].astype(jnp.float32).reshape(16 * PAD, HD)
    level = wide[pl.ds(28, pieces, stride=PAD), :] + wide[pl.ds(29, pieces, stride=PAD), :]
    holder = wide[pl.ds(30, pieces, stride=PAD), :]
    owners[...] = holder
    share = jnp.zeros_like(level)
    for r in range(16):
        member = holder == float(r)
        peak = jnp.max(jnp.where(member, level, NEG), axis=0, keepdims=True)
        expo = jnp.where(member, jnp.exp(jnp.where(member, level - peak, 0.0)), 0.0)
        share = share + expo * (1.0 / jnp.sum(expo, axis=0, keepdims=True))
    turned = share.T
    for b in range(pieces):
        block = slice(b * PAD, (b + 1) * PAD)
        wide[block] = wide[block] * turned[0:PAD, b : b + 1]

    def join_half(part, to):
        def join(i, carry):
            r = part * 8 + i
            mine = r.astype(jnp.float32)
            first_row = pl.multiple_of((held + r) * PAD, PAD)
            total = wide[pl.ds(first_row, PAD), :]
            for b in range(held):
                total = total + jnp.where(
                    owners[b : b + 1] == mine, wide[b * PAD : (b + 1) * PAD], 0.0
                )
            joined[i] = total
            return carry

        lax.fori_loop(0, 8, join, 0)
        for i in range(8):
            compact[pl.ds(i, tree_size, stride=8), :] = joined[i, 0:tree_size]
        attn[to, me] = compact[...].astype(jnp.bfloat16)

    last = [GridGather(attn.at[c], send3, recv3, c) for c in range(2)]
    join_half(1 - tp, 0)
    last[0].begin()
    join_half(tp, 1)
    last[1].begin()
    last[0].along(1)
    last[1].along(1)
    last[0].across(0)
    last[0].along(2)
    last[1].across(0)
    last[1].along(2)
    last[0].across(1)
    last[0].along(3)
    last[1].across(1)
    last[1].along(3)
    last[0].across(2)
    last[0].across(3)
    last[1].across(2)
    loads[7].wait()

    def project(part):
        total = jnp.zeros(half_out.shape, jnp.float32)
        for kv in range(4):
            for g in range(0, 4, 2):
                head = 4 * kv + g
                pair = jnp.concatenate(
                    [attn[part, 4 * g + kv], attn[part, 4 * g + 4 + kv]], axis=1
                )
                total = total + jnp.dot(
                    pair, weight_v[head * HD : (head + 2) * HD],
                    preferred_element_type=jnp.float32,
                )
        return total

    last[0].end()
    last[1].across(3)
    half_out[...] = project(0).astype(jnp.bfloat16)
    swap = pltpu.make_async_remote_copy(
        src_ref=half_out,
        dst_ref=half_in,
        send_sem=send4,
        recv_sem=recv4,
        device_id={"tp": 1 - tp},
        device_id_type=MESH,
    )
    swap.start()
    last[1].end()
    own_half = project(1)
    swap.wait_recv()
    mixed_ref[...] = (own_half + half_in[...].astype(jnp.float32)).astype(jnp.bfloat16)

    swap.wait_send()
    for hop in hops:
        hop.wait_send()
    for gather in last:
        gather.finish()
    for k, target, remote in sent:
        if k == 0:

            @pl.when(target != me)
            def _():
                remote().wait_send()

        else:
            remote().wait_send()


def append_kernel(
    owner_h, len_h, path_h, cache_ref, rows_h, out_ref,
    owner_ref, len_ref, path_ref, rows_ref, sems, *held,
):
    slots, piece_rows, width = cache_ref.shape
    span = 32
    loads = [pltpu.make_async_copy(cache_ref.at[s], held[s], sems.at[s]) for s in range(slots)]
    stores = [
        pltpu.make_async_copy(held[s], out_ref.at[s], sems.at[slots + s]) for s in range(slots)
    ]
    pairs = [(owner_h, owner_ref), (len_h, len_ref), (path_h, path_ref), (rows_h, rows_ref)]
    small = [
        pltpu.make_async_copy(there, here, sems.at[2 * slots + n])
        for n, (there, here) in enumerate(pairs)
    ]
    for load in small + loads:
        load.start()
    for load in small:
        load.wait()
    for s in range(slots):
        request = jnp.maximum(owner_ref[0, s], 0)
        begin = len_ref[request] - owner_ref[1, s] * piece_rows
        start = pl.multiple_of(jnp.clip(begin, 0, piece_rows - span) // 16 * 16, 16)
        count = jnp.int32(0)
        for j in range(path_ref.shape[0]):
            count = count + (path_ref[j, request] >= 0).astype(jnp.int32)
        count = jnp.where(owner_ref[0, s] >= 0, count, 0)
        offset = iota((span, 16), 0) + (start - begin)
        lane = iota((span, 16), 1) - 12
        low = ((offset == lane) & (lane >= 0)).astype(jnp.bfloat16)
        high = ((offset == lane + 4) & (lane >= 0)).astype(jnp.bfloat16)
        chosen = jnp.dot(
            low, rows_ref[s, :, :width], preferred_element_type=jnp.float32
        ) + jnp.dot(high, rows_ref[s, :, width:], preferred_element_type=jnp.float32)
        offset = iota((span, width), 0) + (start - begin)
        writing = (offset >= 0) & (offset < count)
        loads[s].wait()
        near = held[s][pl.ds(start, span), :].astype(jnp.float32)
        held[s][pl.ds(start, span), :] = jnp.where(writing, chosen, near).astype(jnp.bfloat16)
        stores[s].start()
    for store in stores:
        store.wait()


def shards_grid(
    queries, tree_kv, tree_parent, accepted_path, cache_kv, piece_owner, cache_len, out_weight
):
    slots, piece_rows, width = cache_kv.shape
    tree_size = queries.shape[1]
    columns = queries.shape[2]
    reqs = 16
    half = reqs * tree_size // 2
    vmem = pl.BlockSpec(memory_space=pltpu.VMEM)
    hbm = pl.BlockSpec(memory_space=pltpu.HBM)
    pieces = reqs * (slots + 1)
    dma = pltpu.SemaphoreType.DMA
    bf16, f32, i32 = jnp.bfloat16, jnp.float32, jnp.int32
    owner_t, path_t = piece_owner.T, accepted_path.T
    mixed, rows = pl.pallas_call(
        layer_kernel,
        out_shape=(
            jax.ShapeDtypeStruct((half, out_weight.shape[1]), bf16),
            jax.ShapeDtypeStruct((slots, 16, columns), bf16),
        ),
        in_specs=[hbm] * 8,
        out_specs=(vmem, vmem),
        scratch_shapes=[
            pltpu.SMEM(owner_t.shape, i32),
            pltpu.VMEM(owner_t.shape, i32),
            pltpu.SMEM(cache_len.shape, i32),
            pltpu.VMEM(tree_parent.shape, i32),
            pltpu.VMEM(path_t.shape, i32),
            pltpu.VMEM(queries.shape, bf16),
            pltpu.VMEM(tree_kv.shape, bf16),
            pltpu.VMEM(cache_kv.shape, bf16),
            pltpu.VMEM(out_weight.shape, bf16),
            pltpu.VMEM((reqs, PAD, HD), bf16),
            pltpu.VMEM((reqs, PAD, HD), bf16),
            pltpu.VMEM((reqs, 1, 128), i32),
            pltpu.SMEM((reqs, 1, 128), i32),
            pltpu.VMEM((reqs - 1, slots * PAD, HD), bf16),
            pltpu.VMEM((reqs, slots * PAD, HD), bf16),
            pltpu.VMEM((PAD, columns), f32),
            pltpu.VMEM((PAD, width), f32),
            pltpu.VMEM((PAD, width), bf16),
            pltpu.VMEM((PAD, PAD), f32),
            pltpu.VMEM((4, 4, slots * PAD, HD), bf16),
            pltpu.VMEM((reqs, slots * PAD, HD), bf16),
            pltpu.VMEM((reqs, PAD, HD), bf16),
            pltpu.VMEM((reqs, PAD, HD), bf16),
            pltpu.VMEM((pieces * PAD, HD), f32),
            pltpu.VMEM((pieces, HD), f32),
            pltpu.VMEM((reqs // 2, PAD, HD), f32),
            pltpu.VMEM((half, HD), f32),
            pltpu.VMEM((2, reqs, half, HD), bf16),
            pltpu.VMEM((half, out_weight.shape[1]), bf16),
            pltpu.VMEM((half, out_weight.shape[1]), bf16),
            dma((10,)),
            dma((reqs,)),
            dma((reqs,)),
            dma((reqs,)),
            dma((reqs,)),
            dma((reqs,)),
            dma((reqs,)),
            dma((reqs,)),
            dma((reqs,)),
            dma((4, 4)),
            dma((reqs,)),
            dma((2, KINDS)),
            dma((2, KINDS)),
            dma,
            dma,
        ],
        compiler_params=pltpu.CompilerParams(
            collective_id=0, has_side_effects=True, vmem_limit_bytes=VMEM_LIMIT
        ),
    )(owner_t, cache_len, tree_parent, path_t, queries, tree_kv, cache_kv, out_weight)
    cache_out = pl.pallas_call(
        append_kernel,
        out_shape=jax.ShapeDtypeStruct(cache_kv.shape, bf16),
        in_specs=[hbm] * 5,
        out_specs=hbm,
        scratch_shapes=[
            pltpu.SMEM(owner_t.shape, i32),
            pltpu.SMEM(cache_len.shape, i32),
            pltpu.SMEM(path_t.shape, i32),
            pltpu.VMEM((slots, 16, columns), bf16),
            dma((2 * slots + 4,)),
        ]
        + [pltpu.VMEM(cache_kv.shape[1:], bf16)] * slots,
        compiler_params=pltpu.CompilerParams(vmem_limit_bytes=VMEM_LIMIT),
    )(owner_t, cache_len, path_t, cache_kv, rows)
    mixed = mixed.reshape(tree_size, reqs // 2, out_weight.shape[1]).transpose(1, 0, 2)
    return mixed, cache_out


def solution(mesh):
    body = shards_grid if dict(mesh.shape) == {"req": 16, "tp": 2} else shards_general
    return jax.shard_map(
        body,
        mesh=mesh,
        in_specs=(
            P("req", None, "tp"),
            P("req", None, "tp"),
            P("req", None),
            P(),
            P("req", None, "tp"),
            P("req", None),
            P(),
            P("tp", "req"),
        ),
        out_specs=(P("tp", None, "req"), P("req", None, "tp")),
        check_vma=False,
    )
```
